256 devices in a mesh: space: 16 (over x, y), tm: 16 (over z, core).
Axes of the slice: x: 4, y: 4, z: 8, core: 2. Of those that a mesh axis runs over, the one named last changes fastest.
Arguments:
- start: float32 [1024, 65536], P('tm', 'space'), may hold values from -3 to 3
- right_side: float32 [1024, 65536], P('tm', 'space'), may hold values from -12 to 12
- noise: float32 [65536], P('space'), may hold values from 0.5 to 2
- tile_ids: int32 [512, 4], P('space'), may hold values from 0 to 511, as said below
- space_tiles: float32 [512, 4, 128, 128], P('space'), may hold values from -1 to 2
- time_kernel: float32 [1024, 1024], P('tm'), may hold values from -1 to 2
Outputs:
- next_iterate: float32 [1024, 65536], P('tm', 'space')
- next_residual: float32 [1024, 65536], P('tm', 'space')
The draws below stay inside these ranges and needn't reach their ends.
Inputs may be any that keep to these rules, and one draw needn't show every extreme that they name: tile_ids[t, 0] = t; the other 3 entries of row t are distinct tiles other than t within the (5) consecutive tiles from max(0, min(t - 2, 507)); tiles are in space-filling-curve order.
All inputs are finite; a program needn't handle non-finite values.
Results may differ from the reference program's by a relative error of at most 0.0003.
Values sent between devices are 32-bit elements; how exact they have to be, the bound alone decides.
No kernel may reach another device: no remote copies, remote signals or barrier semaphores. Data moves between devices by JAX's collectives and lax.ppermute only.
A program may use at most 64 MiB of HBM per device.

```python
import math
import jax
import jax.numpy as jnp
from jax import lax

TILE = 128
NB = 4
REACH = 2
HOURS = 1024
TILES_DEV = 32
TILES = 512
SITES = 65536
N_SPACE = 16


def draw_right_side(key, part):
    key = jax.random.fold_in(key, 7)
    site_pos = jnp.arange(SITES, dtype=jnp.float32)[None, :] / SITES
    hour_pos = jnp.arange(HOURS, dtype=jnp.float32)[:, None] / HOURS
    scale = jnp.sqrt((1.0 + 2.0 * site_pos) * (1.0 + 2.0 * hour_pos))
    values = jax.random.truncated_normal(key, -3.0, 3.0, (HOURS, SITES), jnp.float32)
    return (values * scale).astype(jnp.float32)


def draw_tile_ids(key, part):
    key = jax.random.fold_in(key, 11)
    tiles_all = jnp.arange(TILES, dtype=jnp.int32)
    lowest = jnp.clip(tiles_all - REACH, 0, TILES - 1 - 2 * REACH)
    others = lowest[:, None] + jnp.arange(2 * REACH, dtype=jnp.int32)[None, :]
    others = others + (others >= tiles_all[:, None]).astype(jnp.int32)
    scores = jax.random.randint(key, (TILES, 2 * REACH), 0, 1048576) * 8 + jnp.arange(2 * REACH, dtype=jnp.int32)[None, :]
    order = jnp.argsort(scores, axis=1, stable=True)
    picked = jnp.take_along_axis(others, order, axis=1)[:, :NB - 1]
    return jnp.concatenate([tiles_all[:, None], picked], axis=1).astype(jnp.int32)


def draw_space_tiles(key, part):
    key = jax.random.fold_in(key, 12)
    key_off, key_diag = jax.random.split(key)
    bound = 0.95 * 2.0 / ((NB + 4 * REACH + 1) * TILE)
    spread = jax.random.uniform(key_off, (TILES, NB, TILE, TILE), jnp.float32, -1.0, 1.0)
    off_part = bound * spread
    diagonal = jax.random.uniform(key_diag, (TILES, TILE), jnp.float32, 1.0, 2.0)
    eye_mask = jnp.arange(TILE)[:, None] == jnp.arange(TILE)[None, :]
    own_mask = (jnp.arange(NB) == 0)[None, :, None, None] & eye_mask[None, None, :, :]
    return jnp.where(own_mask, diagonal[:, None, :, None], off_part).astype(jnp.float32)


def draw_time_kernel(key, part):
    key = jax.random.fold_in(key, 13)
    key_off, key_diag = jax.random.split(key)
    spread = jax.random.uniform(key_off, (HOURS, HOURS), jnp.float32, -1.0, 1.0)
    off_part = (spread + spread.T) * (0.45 / HOURS)
    diagonal = jax.random.uniform(key_diag, (HOURS,), jnp.float32, 1.0, 2.0)
    eye_mask = jnp.arange(HOURS)[:, None] == jnp.arange(HOURS)[None, :]
    return jnp.where(eye_mask, diagonal[:, None], off_part).astype(jnp.float32)


def block_scale(stream_key, dims, pieces, low, high):
    level, own = 1.0, jax.random.fold_in(stream_key, 6)
    for axis_at, blocks in pieces:
        steps = jnp.exp(jax.random.uniform(jax.random.fold_in(own, axis_at), (blocks,), jnp.float32, low / len(pieces), high / len(pieces)))
        level = level * jnp.repeat(steps, dims[axis_at] // blocks).reshape([-1 if axis == axis_at else 1 for axis in range(len(dims))])
    return level


def normal_values(stream_key, shape, scale, most, shards=(), kind=jnp.bfloat16):
    array = scale * jax.random.normal(stream_key, shape, jnp.float32)
    if shards:
        array = array * block_scale(stream_key, shape, shards, -0.22, 0.18)
    return jnp.clip(array, -most, most).astype(kind)


def setup_inputs(seed: int = 0) -> dict:
    key_list = jax.random.split(jax.random.key(seed), 7)
    start = normal_values(key_list[0], (HOURS, SITES), 0.5, 3.0, ((0, 16), (1, 16)), jnp.float32)
    right_side = draw_right_side(jax.random.fold_in(key_list[6], 71), 0)
    noise = jnp.clip(jnp.exp(math.log(2.0) - 1.3862944 * jax.random.uniform(key_list[2], (SITES,), jnp.float32) ** block_scale(key_list[2], (SITES,), ((0, 16),), -0.2, 0.2)), 0.5, 2.0)
    tile_ids = draw_tile_ids(jax.random.fold_in(key_list[6], 71), 0)
    space_tiles = draw_space_tiles(jax.random.fold_in(key_list[6], 71), 0)
    time_kernel = draw_time_kernel(jax.random.fold_in(key_list[6], 71), 0)
    return {"start": start, "right_side": right_side, "noise": noise, "tile_ids": tile_ids, "space_tiles": space_tiles, "time_kernel": time_kernel}


def space_apply(field, tile_ids, space_tiles):
    blocks = field.reshape(HOURS, TILES, TILE)

    def one_group(pair):
        ids_group, tiles_group = pair
        gathered = jnp.take(blocks, ids_group, axis=1)
        return jnp.einsum("htnc,tnrc->htr", gathered, tiles_group, precision=lax.Precision.HIGHEST)

    stacked = lax.map(one_group, (tile_ids.reshape(N_SPACE, TILES_DEV, NB), space_tiles.reshape(N_SPACE, TILES_DEV, NB, TILE, TILE)))
    return jnp.transpose(stacked, (1, 0, 2, 3)).reshape(HOURS, SITES)


def operate(field, noise, tile_ids, space_tiles, time_kernel):
    spatial = space_apply(field, tile_ids, space_tiles)
    return jnp.dot(time_kernel, spatial, precision=lax.Precision.HIGHEST) + noise[None, :] * field


def reference(start, right_side, noise, tile_ids, space_tiles, time_kernel):
    residual = right_side - operate(start, noise, tile_ids, space_tiles, time_kernel)
    image = operate(residual, noise, tile_ids, space_tiles, time_kernel)
    norm_sum = jnp.sum(residual * residual)
    curve_sum = jnp.sum(residual * image)
    alpha = norm_sum / curve_sum
    return start + alpha * residual, residual - alpha * image
```

```python
import jax
import jax.numpy as jnp
from jax import lax
from jax.experimental import pallas as pl
from jax.experimental.pallas import tpu as pltpu
from jax.sharding import PartitionSpec as P

REACH = 2
TILE = 128
CHIPS = 8
SIDE = 4
ORIGIN = (0, 4, 6, 2, 1, 5, 7, 3)
PLACE = {origin: j for j, origin in enumerate(ORIGIN)}
SHIFTS = (1, 7, 2, 6, 4, 3, 5)
SWAP = [(i, i ^ 1) for i in range(2 * CHIPS)]
F32 = jnp.float32
BF16 = jnp.bfloat16
VMEM = pl.BlockSpec(memory_space=pltpu.VMEM)
SMEM = pl.BlockSpec(memory_space=pltpu.SMEM)


def along_z(shift):
    return [(z * 2 + c, (z + shift) % CHIPS * 2 + c) for z in range(CHIPS) for c in range(2)]


def halves(value):
    high = value.astype(BF16)
    return high, (value - high.astype(F32)).astype(BF16)


def params(megabytes):
    return pltpu.CompilerParams(vmem_limit_bytes=megabytes * 1024 * 1024)


def cost(flops, moved):
    return pl.CostEstimate(flops=flops, bytes_accessed=moved, transcendentals=0)


def dot_nt(a, b):
    return lax.dot_general(a, b, (((1,), (1,)), ((), ())), preferred_element_type=F32)


def dot_nn(a, b):
    return lax.dot_general(a, b, (((1,), (0,)), ((), ())), preferred_element_type=F32)


def space_wide_kernel(at_ref, ids_ref, low_ref, x_ref, high_ref, tiles_ref, out_ref, win_ref):
    step = pl.program_id(0)
    hours = x_ref.shape[0]

    @pl.when(step == 0)
    def _():
        count = x_ref.shape[1] // TILE
        for i in range(count + 2 * REACH):
            if i < REACH:
                piece = low_ref[:, i * TILE : (i + 1) * TILE]
            elif i < count + REACH:
                piece = x_ref[:, (i - REACH) * TILE : (i - REACH + 1) * TILE]
            else:
                j = i - count - REACH
                piece = high_ref[:, j * TILE : (j + 1) * TILE]
            high, low = halves(piece)
            win_ref[i, :hours, :] = high
            win_ref[i, hours:, :] = low

    group = (at_ref[0] + step) % CHIPS
    rows = tiles_ref.shape[0]
    for i in range(rows):
        whi, wlo = halves(tiles_ref[i])
        total = None
        for n in range(whi.shape[0]):
            both = win_ref[ids_ref[group * rows + i, n] - at_ref[1]]
            a = dot_nt(both, whi[n])
            b = dot_nt(both[:hours], wlo[n])
            part = a[:hours] + a[hours:] + b
            total = part if total is None else total + part
        out_ref[0, :, i * TILE : (i + 1) * TILE] = total


def space_wide(at, ids, low, x, high, tiles):
    hours, sites = x.shape
    count, nb = ids.shape
    rows = count // CHIPS
    grid_spec = pltpu.PrefetchScalarGridSpec(
        num_scalar_prefetch=2,
        grid=(CHIPS,),
        in_specs=[
            pl.BlockSpec(low.shape, lambda d, at, ids: (0, 0)),
            pl.BlockSpec(x.shape, lambda d, at, ids: (0, 0)),
            pl.BlockSpec(high.shape, lambda d, at, ids: (0, 0)),
            pl.BlockSpec((rows, nb, TILE, TILE), lambda d, at, ids: ((at[0] + d) % CHIPS, 0, 0, 0)),
        ],
        out_specs=pl.BlockSpec((1, hours, rows * TILE), lambda d, at, ids: (d, 0, 0)),
        scratch_shapes=[pltpu.VMEM((count + 2 * REACH, 2 * hours, TILE), BF16)],
    )
    return pl.pallas_call(
        space_wide_kernel,
        grid_spec=grid_spec,
        out_shape=jax.ShapeDtypeStruct((CHIPS, hours, rows * TILE), F32),
        compiler_params=params(24),
        cost_estimate=cost(3 * 2 * hours * sites * nb * TILE, 10 << 20),
        name="space_wide",
    )(at, ids, low, x, high, tiles)


def space_mixed_kernel(at_ref, ids_ref, left_ref, own_ref, right_ref, tiles_ref, out_ref, hi_ref, lo_ref):
    step = pl.program_id(0)
    hours = own_ref.shape[1]
    rows = own_ref.shape[2] // TILE

    @pl.when(step == 0)
    def _():
        for j in range(CHIPS):
            at_left = PLACE[(ORIGIN[j] + 1) % CHIPS]
            at_right = PLACE[(ORIGIN[j] - 1) % CHIPS]
            for i in range(rows + 2 * REACH):
                if i < REACH:
                    piece = left_ref[at_left, :, i * TILE : (i + 1) * TILE]
                elif i < rows + REACH:
                    piece = own_ref[j, :, (i - REACH) * TILE : (i - REACH + 1) * TILE]
                else:
                    k = i - rows - REACH
                    piece = right_ref[at_right, :, k * TILE : (k + 1) * TILE]
                high, low = halves(piece)
                hi_ref[i, j * hours : (j + 1) * hours, :] = high
                lo_ref[i, j * hours : (j + 1) * hours, :] = low

    whi, wlo = halves(tiles_ref[0])
    total = None
    for n in range(whi.shape[0]):
        i = ids_ref[at_ref[0] * rows + step, n] - at_ref[2]
        high, low = hi_ref[i], lo_ref[i]
        part = dot_nt(high, whi[n]) + (dot_nt(high, wlo[n]) + dot_nt(low, whi[n]))
        total = part if total is None else total + part
    out_ref[...] = total.reshape(out_ref.shape)


def space_mixed(at, ids, left, own, right, tiles):
    count, nb = ids.shape
    rows = count // CHIPS
    hours = own.shape[1]
    whole = lambda i, at, ids: (0, 0, 0)
    grid_spec = pltpu.PrefetchScalarGridSpec(
        num_scalar_prefetch=2,
        grid=(rows,),
        in_specs=[
            pl.BlockSpec(left.shape, whole),
            pl.BlockSpec(own.shape, whole),
            pl.BlockSpec(right.shape, whole),
            pl.BlockSpec((1, nb, TILE, TILE), lambda i, at, ids: (at[0] * rows + i, 0, 0, 0)),
        ],
        out_specs=pl.BlockSpec((CHIPS, hours, TILE), lambda i, at, ids: (0, 0, i)),
        scratch_shapes=[pltpu.VMEM((rows + 2 * REACH, CHIPS * hours, TILE), BF16)] * 2,
    )
    return pl.pallas_call(
        space_mixed_kernel,
        grid_spec=grid_spec,
        out_shape=jax.ShapeDtypeStruct(own.shape, F32),
        compiler_params=params(24),
        cost_estimate=cost(3 * 2 * own.size * nb * TILE, 5 << 20),
        name="space_mixed",
    )(at, ids, left, own, right, tiles)


def time_rows_kernel(at_ref, *refs):
    strips, (hi_ref, lo_ref) = refs[:-2], refs[-2:]
    rows, half = strips[0].shape[1:]
    for side in range(2):
        for k in range(SIDE):
            row = pl.multiple_of((at_ref[3 + side] + k) % SIDE * rows, rows)
            high, low = halves(strips[side * SIDE + k][...])
            hi_ref[:, pl.ds(row, rows), side * half : (side + 1) * half] = high
            lo_ref[:, pl.ds(row, rows), side * half : (side + 1) * half] = low


def time_rows(at, strips):
    chips, rows, half = strips[0].shape
    shape = jax.ShapeDtypeStruct((chips, rows * SIDE, 2 * half), BF16)
    return pl.pallas_call(
        time_rows_kernel,
        in_specs=[SMEM] + [VMEM] * len(strips),
        out_specs=(VMEM, VMEM),
        out_shape=(shape, shape),
        compiler_params=params(16),
        cost_estimate=cost(1 << 20, 4 << 20),
        name="time_rows",
    )(at, *strips)


def split_hours(at_ref, own_ref, other_ref, uhi_ref, ulo_ref):
    hours = own_ref.shape[1]
    for j in range(CHIPS):
        chip = (at_ref[0] + ORIGIN[j]) % CHIPS
        for ref, core in ((own_ref, at_ref[1]), (other_ref, 1 - at_ref[1])):
            row = pl.multiple_of((2 * chip + core) * hours, hours)
            high, low = halves(ref[j])
            uhi_ref[pl.ds(row, hours), :] = high
            ulo_ref[pl.ds(row, hours), :] = low


def time_product(khi_ref, klo_ref, uhi_ref, ulo_ref, columns):
    chips, hours, depth = khi_ref.shape
    khi = khi_ref[...].reshape(chips * hours, depth)
    klo = klo_ref[...].reshape(chips * hours, depth)
    uhi, ulo = uhi_ref[:, columns], ulo_ref[:, columns]
    return dot_nn(khi, uhi) + (dot_nn(khi, ulo) + dot_nn(klo, uhi))


def residual_kernel(at_ref, khi_ref, klo_ref, own_ref, other_ref, *refs):
    known, (out_ref, uhi_ref, ulo_ref) = refs[:CHIPS], refs[CHIPS:]
    chips, hours, sites = out_ref.shape
    split_hours(at_ref, own_ref, other_ref, uhi_ref, ulo_ref)
    width = sites // 2
    for part in range(2):
        columns = slice(part * width, (part + 1) * width)
        mixed = time_product(khi_ref, klo_ref, uhi_ref, ulo_ref, columns).reshape(chips, hours, width)
        for j in range(chips):
            out_ref[j, :, columns] = known[j][:, columns] - mixed[j]


def residual_of(at, khi, klo, own, other, known):
    return pl.pallas_call(
        residual_kernel,
        in_specs=[SMEM] + [VMEM] * (4 + CHIPS),
        out_specs=VMEM,
        out_shape=jax.ShapeDtypeStruct(own.shape, F32),
        scratch_shapes=[pltpu.VMEM((2 * CHIPS * own.shape[1], own.shape[2]), BF16)] * 2,
        compiler_params=params(24),
        cost_estimate=cost(3 * 2 * khi.shape[2] * own.size, 6 << 20),
        name="residual_of",
    )(at, khi, klo, own, other, *known)


def image_kernel(at_ref, khi_ref, klo_ref, own_ref, other_ref, r_ref, noise_ref, out_ref, sums_ref, uhi_ref, ulo_ref):
    chips, hours, sites = out_ref.shape
    split_hours(at_ref, own_ref, other_ref, uhi_ref, ulo_ref)
    width = sites // 2
    squares = jnp.zeros((8, TILE), F32)
    curves = jnp.zeros((8, TILE), F32)
    for part in range(2):
        columns = slice(part * width, (part + 1) * width)
        mixed = time_product(khi_ref, klo_ref, uhi_ref, ulo_ref, columns).reshape(chips, hours, width)
        r = r_ref[:, :, columns]
        image = mixed + noise_ref[:, columns][None] * r
        out_ref[:, :, columns] = image
        for t in range(width // TILE):
            cut = slice(t * TILE, (t + 1) * TILE)
            a, b = r[:, :, cut].reshape(-1, 8, TILE), image[:, :, cut].reshape(-1, 8, TILE)
            squares += jnp.sum(a * a, axis=0)
            curves += jnp.sum(a * b, axis=0)
    sums_ref[:8, :] = squares
    sums_ref[8:, :] = curves


def image_of(at, khi, klo, own, other, residual, noise):
    return pl.pallas_call(
        image_kernel,
        in_specs=[SMEM] + [VMEM] * 6,
        out_specs=(VMEM, VMEM),
        out_shape=(jax.ShapeDtypeStruct(own.shape, F32), jax.ShapeDtypeStruct((16, TILE), F32)),
        scratch_shapes=[pltpu.VMEM((2 * CHIPS * own.shape[1], own.shape[2]), BF16)] * 2,
        compiler_params=params(24),
        cost_estimate=cost(3 * 2 * khi.shape[2] * own.size, 6 << 20),
        name="image_of",
    )(at, khi, klo, own, other, residual, noise)


def update_kernel(at_ref, sums_ref, start_ref, *refs):
    residual, image, (iterate_ref, next_ref) = refs[:CHIPS], refs[CHIPS : 2 * CHIPS], refs[2 * CHIPS :]
    alpha = jnp.sum(sums_ref[:8, :]) / jnp.sum(sums_ref[8:, :])
    width = residual[0].shape[1]
    for d in range(CHIPS):
        columns = pl.ds(pl.multiple_of((at_ref[0] + d) % CHIPS * width, width), width)
        r = residual[d][...]
        iterate_ref[:, columns] = start_ref[:, columns] + alpha * r
        next_ref[:, columns] = r - alpha * image[d][...]


def update(at, sums, start, residual, image):
    shape = jax.ShapeDtypeStruct(start.shape, F32)
    return pl.pallas_call(
        update_kernel,
        in_specs=[SMEM] + [VMEM] * (2 + 2 * CHIPS),
        out_specs=(VMEM, VMEM),
        out_shape=(shape, shape),
        compiler_params=params(16),
        cost_estimate=cost(4 * start.size, 5 << 20),
        name="update",
    )(at, sums, start, *residual, *image)


def exchange(blocks):
    got = {0: blocks[0]}
    for shift in SHIFTS:
        got[-shift % CHIPS] = lax.ppermute(blocks[shift], "tm", along_z(shift))
    return got


def local(start, right_side, noise, tile_ids, space_tiles, time_kernel):
    hours_dev, sites_dev = start.shape
    count = tile_ids.shape[0]
    width = sites_dev // CHIPS
    edge = REACH * TILE
    spaces = lax.axis_size("space")
    space, tm = lax.axis_index("space"), lax.axis_index("tm")
    chip, core = tm // 2, tm % 2
    along_x, along_y = space // SIDE, space % SIDE
    at = jnp.stack(
        [chip, core, space * count + chip * (count // CHIPS) - REACH, along_y, along_x]
    ).astype(jnp.int32)
    at_wide = jnp.stack([chip, space * count - REACH]).astype(jnp.int32)

    forward = [(i, i + 1) for i in range(spaces - 1)]
    backward = [(target, source) for source, target in forward]
    low = lax.ppermute(start[:, sites_dev - edge :], "space", forward)
    high = lax.ppermute(start[:, :edge], "space", backward)

    rows, half = time_kernel.shape[0] // SIDE, time_kernel.shape[1] // 2
    strip = jnp.stack(
        [
            lax.dynamic_slice(time_kernel, (along_y * rows, 0), (rows, half)),
            lax.dynamic_slice(time_kernel, (along_x * rows, half), (rows, half)),
        ]
    )[:, None]
    for shift in (4, 2, -1):
        strip = jnp.concatenate([strip, lax.ppermute(strip, "tm", along_z(shift))], axis=1)
    strips = [strip[0]]
    for k in range(1, SIDE):
        pairs = [(a * SIDE + b, a * SIDE + (b - k) % SIDE) for a in range(SIDE) for b in range(SIDE)]
        strips.append(lax.ppermute(strip[0], "space", pairs))
    strips.append(strip[1])
    for k in range(1, SIDE):
        pairs = [(a * SIDE + b, (a - k) % SIDE * SIDE + b) for a in range(SIDE) for b in range(SIDE)]
        strips.append(lax.ppermute(strip[1], "space", pairs))
    khi, klo = time_rows(at, strips)

    def known(d):
        first = (chip + d) % CHIPS * width
        cut = lambda a: lax.dynamic_slice(a, (0, first), (hours_dev, width))
        return cut(right_side) - lax.dynamic_slice(noise, (first,), (width,))[None, :] * cut(start)

    q = exchange([known(d) for d in range(CHIPS)])
    u = space_wide(at_wide, tile_ids, low, start, high, space_tiles)
    u = exchange([u[d] for d in range(CHIPS)])
    own = jnp.stack([u[o] for o in ORIGIN])
    other = lax.ppermute(own, "tm", SWAP)
    residual = residual_of(at, khi, klo, own, other, [q[o] for o in ORIGIN])

    n_tm = 2 * CHIPS
    up, down = [], []
    for s in range(spaces):
        for z in range(CHIPS):
            for c in range(2):
                source, target = (s * CHIPS + z), (s * CHIPS + z + 1)
                if target < spaces * CHIPS:
                    up.append((source * 2 + c, target * 2 + c))
                    down.append((target * 2 + c, source * 2 + c))
    left = lax.ppermute(residual[:, :, width - edge :], ("space", "tm"), up)
    right = lax.ppermute(residual[:, :, :edge], ("space", "tm"), down)
    mixed = space_mixed(at, tile_ids, left, residual, right, space_tiles)
    other = lax.ppermute(mixed, "tm", SWAP)
    noise_here = lax.dynamic_slice(noise, (chip * width,), (width,))[None, :]
    image, sums = image_of(at, khi, klo, mixed, other, residual, noise_here)

    sums = sums + lax.ppermute(sums, "tm", SWAP)
    for shift in (4, 2, 1):
        sums = sums + lax.ppermute(sums, "tm", along_z(shift))
    for k in (2, 1):
        pairs = [(a * SIDE + b, a * SIDE + (b + k) % SIDE) for a in range(SIDE) for b in range(SIDE)]
        sums = sums + lax.ppermute(sums, "space", pairs)
    for k in (2, 1):
        pairs = [(a * SIDE + b, (a + k) % SIDE * SIDE + b) for a in range(SIDE) for b in range(SIDE)]
        sums = sums + lax.ppermute(sums, "space", pairs)

    back_r = exchange([residual[PLACE[d]] for d in range(CHIPS)])
    back_p = exchange([image[PLACE[d]] for d in range(CHIPS)])
    return update(
        at, sums, start, [back_r[d] for d in range(CHIPS)], [back_p[d] for d in range(CHIPS)]
    )


def solution(mesh):
    placed = (
        P("tm", "space"),
        P("tm", "space"),
        P("space"),
        P("space", None),
        P("space", None, None, None),
        P("tm", None),
    )
    return jax.shard_map(
        local,
        mesh=mesh,
        in_specs=placed,
        out_specs=(P("tm", "space"), P("tm", "space")),
        check_vma=False,
    )
```

```python
import jax
import jax.numpy as jnp
from jax import lax
from jax.experimental import pallas as pl
from jax.experimental.pallas import tpu as pltpu
from jax.sharding import PartitionSpec as P

REACH = 2
TILE = 128
CHIPS = 8
SAME_CORE = [[chip * 2 + core for chip in range(CHIPS)] for core in range(2)]
SIDE = 4
ORIGIN = (0, 4, 6, 2, 1, 5, 7, 3)
SWAP = [(i, i ^ 1) for i in range(2 * CHIPS)]
F32 = jnp.float32
BF16 = jnp.bfloat16
VMEM = pl.BlockSpec(memory_space=pltpu.VMEM)
SMEM = pl.BlockSpec(memory_space=pltpu.SMEM)
ANY = pl.BlockSpec(memory_space=pl.ANY)
HBM = pl.BlockSpec(memory_space=pltpu.HBM)


def along_z(shift):
    return [(z * 2 + c, (z + shift) % CHIPS * 2 + c) for z in range(CHIPS) for c in range(2)]


def halves(value):
    high = value.astype(BF16)
    return high, (value - high.astype(F32)).astype(BF16)


def params(megabytes):
    return pltpu.CompilerParams(vmem_limit_bytes=megabytes * 1024 * 1024)


def cost(flops, moved):
    return pl.CostEstimate(flops=flops, bytes_accessed=moved, transcendentals=0)


def dot_nt(a, b):
    return lax.dot_general(a, b, (((1,), (1,)), ((), ())), preferred_element_type=F32)


def dot_nn(a, b):
    return lax.dot_general(a, b, (((1,), (0,)), ((), ())), preferred_element_type=F32)


def stacked_halves(tiles):
    high, low = halves(tiles)
    return jnp.concatenate([high, low], axis=-2)


def weights_kernel(at_ref, tiles_ref, out_ref):
    out_ref[...] = stacked_halves(tiles_ref[...])


def weights_of(at, tiles):
    count, nb = tiles.shape[:2]
    rows = count // CHIPS
    return pl.pallas_call(
        weights_kernel,
        grid_spec=pltpu.PrefetchScalarGridSpec(
            num_scalar_prefetch=1,
            grid=(rows,),
            in_specs=[pl.BlockSpec((1, nb, TILE, TILE), lambda i, at: (at[0] * rows + i, 0, 0, 0))],
            out_specs=pl.BlockSpec((1, nb, 2 * TILE, TILE), lambda i, at: (i, 0, 0, 0)),
        ),
        out_shape=jax.ShapeDtypeStruct((rows, nb, 2 * TILE, TILE), BF16),
        compiler_params=params(56),
        cost_estimate=cost(0, 0),
        name="weights_of",
    )(at, tiles)


def space_wide_kernel(first, at_ref, ids_ref, edge_ref, noise_ref, x_ref, tiles_ref, right_ref, *refs):
    out_ref, win_ref, x_here, tile_ref, right_here, stage_ref, x_sems, tile_sems, right_sems, out_sems = refs[-10:]
    hours, sites = x_ref.shape
    groups = stage_ref.shape[0]
    rows, nb = tile_ref.shape[0] // groups, tile_ref.shape[1]
    width = rows * TILE
    count = sites // TILE
    needed = range(first * rows, (first + groups) * rows + 2 * REACH)
    inside = [i - REACH for i in needed if 0 <= i - REACH < count]
    pieces = range(inside[0] // rows, inside[-1] // rows + 1)
    place = lambda g: slice(g * width, (g + 1) * width)
    fetch = [pltpu.make_async_copy(x_ref.at[:, place(g)], x_here.at[:, place(g)], x_sems.at[g]) for g in pieces]
    tiles = [
        pltpu.make_async_copy(tiles_ref.at[first * rows + k], tile_ref.at[k], tile_sems.at[k])
        for k in range(rows * groups)
    ]
    right = [
        pltpu.make_async_copy(right_ref.at[:, place(first + k)], right_here.at[k], right_sems.at[k]) for k in range(groups)
    ]
    for copy in fetch + tiles + right:
        copy.start()
    for copy in fetch:
        copy.wait()
    for k, i in enumerate(needed):
        if i < REACH:
            piece = edge_ref[:, i * TILE : (i + 1) * TILE]
        elif i < count + REACH:
            piece = x_here[:, (i - REACH) * TILE : (i - REACH + 1) * TILE]
        else:
            j = i - count - REACH
            piece = edge_ref[:, j * TILE : (j + 1) * TILE]
        high, low = halves(piece)
        win_ref[k, :hours, :] = high
        win_ref[k, hours:, :] = low
    sent = []
    for k in range(groups):
        for i in range(rows):
            tiles[k * rows + i].wait()
        for i in range(rows):
            row = (first + k) * rows + i
            field = [win_ref[ids_ref[n, row] - at_ref[3] - first * rows] for n in range(nb)]
            mine = jnp.concatenate([tile_ref[k * rows + i, n] for n in range(nb)], axis=1)
            product = dot_nt(jnp.concatenate(field, axis=1), stacked_halves(mine))
            columns = slice(i * TILE, (i + 1) * TILE)
            stage_ref[k, :hours, columns] = product[:hours, :TILE] + (product[:hours, TILE:] + product[hours:, :TILE])
        right[k].wait()
        stage_ref[k, hours:, :] = right_here[k] - noise_ref[:, place(first + k)] * x_here[:, place(first + k)]
        sent.append(pltpu.make_async_copy(stage_ref.at[k], out_ref.at[first + k], out_sems.at[k]))
        sent[-1].start()
    for copy in sent:
        copy.wait()


def space_wide(first, at, ids, edge, x, tiles, right_side, noise, begun, after):
    hours, sites = x.shape
    nb, count = ids.shape
    rows, groups = count // CHIPS, CHIPS // 2
    more = ([] if begun is None else [begun]) + after
    return pl.pallas_call(
        lambda *refs: space_wide_kernel(first, *refs),
        in_specs=[SMEM] * 2 + [VMEM] * 2 + [HBM] * 3 + [ANY] * len(more),
        out_specs=ANY,
        out_shape=jax.ShapeDtypeStruct((CHIPS, 2 * hours, rows * TILE), F32),
        input_output_aliases={} if begun is None else {7: 0},
        scratch_shapes=[
            pltpu.VMEM((count // 2 + 2 * REACH, 2 * hours, TILE), BF16),
            pltpu.VMEM((hours, sites), F32),
            pltpu.VMEM((rows * groups, nb, TILE, TILE), F32),
            pltpu.VMEM((groups, hours, rows * TILE), F32),
            pltpu.VMEM((groups, 2 * hours, rows * TILE), F32),
            pltpu.SemaphoreType.DMA((CHIPS,)),
            pltpu.SemaphoreType.DMA((rows * groups,)),
            pltpu.SemaphoreType.DMA((groups,)),
            pltpu.SemaphoreType.DMA((groups,)),
        ],
        compiler_params=params(56),
        cost_estimate=cost(0, 0),
        name="space_wide",
    )(at, ids, edge, noise[None, :], x, tiles, right_side, *more)


def space_mixed_kernel(at_ref, ids_ref, left_ref, own_ref, right_ref, weights_ref, *refs):
    out_ref, hi_ref, lo_ref = refs[-3:]
    rows, nb = weights_ref.shape[:2]
    for i in range(rows + 2 * REACH):
        if i < REACH:
            piece = left_ref[:, :, i * TILE : (i + 1) * TILE]
        elif i < rows + REACH:
            piece = own_ref[:, :, (i - REACH) * TILE : (i - REACH + 1) * TILE]
        else:
            k = i - rows - REACH
            piece = right_ref[:, :, k * TILE : (k + 1) * TILE]
        high, low = halves(piece.reshape(-1, TILE))
        hi_ref[i] = high
        lo_ref[i] = low
    for row in range(rows):
        total = None
        for n in range(nb):
            i = ids_ref[n, at_ref[0] * rows + row] - at_ref[2]
            both = dot_nt(hi_ref[i], weights_ref[row, n])
            part = both[:, :TILE] + (both[:, TILE:] + dot_nt(lo_ref[i], weights_ref[row, n, :TILE]))
            total = part if total is None else total + part
        out_ref[:, :, row * TILE : (row + 1) * TILE] = total.reshape(out_ref.shape[:2] + (TILE,))


def space_mixed(at, ids, left, own, right, weights, after):
    nb, count = ids.shape
    rows, hours = count // CHIPS, own.shape[0] * own.shape[1]
    whole = lambda i, at, ids: (0, 0, 0)
    return pl.pallas_call(
        space_mixed_kernel,
        grid_spec=pltpu.PrefetchScalarGridSpec(
            num_scalar_prefetch=2,
            grid=(1,),
            in_specs=[
                pl.BlockSpec(left.shape, whole),
                pl.BlockSpec(own.shape, whole),
                pl.BlockSpec(right.shape, whole),
                pl.BlockSpec((rows, nb, 2 * TILE, TILE), lambda i, at, ids: (0, 0, 0, 0)),
            ]
            + [ANY] * len(after),
            out_specs=pl.BlockSpec(own.shape, whole),
            scratch_shapes=[pltpu.VMEM((rows + 2 * REACH, hours, TILE), BF16)] * 2,
        ),
        out_shape=jax.ShapeDtypeStruct(own.shape, F32),
        compiler_params=params(24),
        cost_estimate=cost(0, 0),
        name="space_mixed",
    )(at, ids, left, own, right, weights, *after)


def time_rows_kernel(at_ref, *refs):
    strips, (hi_ref, lo_ref) = refs[:SIDE], refs[SIDE:]
    chips, rows, _ = strips[0].shape
    for k in range(SIDE):
        row = pl.multiple_of((at_ref[4] + k) % SIDE * rows, rows)
        for j in range(chips):
            chip = (at_ref[0] + ORIGIN[j]) % chips
            high, low = halves(strips[k][j])
            hi_ref[chip, pl.ds(row, rows), :] = high
            lo_ref[chip, pl.ds(row, rows), :] = low


def time_rows(at, strips):
    chips, rows, depth = strips[0].shape
    shape = jax.ShapeDtypeStruct((chips, rows * SIDE, depth), BF16)
    return pl.pallas_call(
        time_rows_kernel,
        in_specs=[SMEM] + [VMEM] * SIDE,
        out_specs=(VMEM, VMEM),
        out_shape=(shape, shape),
        compiler_params=params(16),
        cost_estimate=cost(0, 0),
        name="time_rows",
    )(at, *strips)


def split_hours(at_ref, own_ref, other_ref, uhi_ref, ulo_ref):
    hours = other_ref.shape[1]
    for chip in range(CHIPS):
        for ref, core in ((own_ref, at_ref[1]), (other_ref, 1 - at_ref[1])):
            row = pl.multiple_of((2 * chip + core) * hours, hours)
            high, low = halves(ref[chip, :hours, :])
            uhi_ref[pl.ds(row, hours), :] = high
            ulo_ref[pl.ds(row, hours), :] = low


def time_product(khi_ref, klo_ref, uhi_ref, ulo_ref, columns):
    chips, hours, depth = khi_ref.shape
    khi = khi_ref[...].reshape(chips * hours, depth)
    klo = klo_ref[...].reshape(chips * hours, depth)
    uhi, ulo = uhi_ref[:, columns], ulo_ref[:, columns]
    mixed = dot_nn(khi, uhi) + (dot_nn(khi, ulo) + dot_nn(klo, uhi))
    return mixed.reshape(chips, hours, -1)


def residual_kernel(at_ref, khi_ref, klo_ref, got_ref, other_ref, out_ref, uhi_ref, ulo_ref):
    chips, hours, sites = out_ref.shape
    split_hours(at_ref, got_ref, other_ref, uhi_ref, ulo_ref)
    width = sites // 2
    for part in range(2):
        columns = slice(part * width, (part + 1) * width)
        mixed = time_product(khi_ref, klo_ref, uhi_ref, ulo_ref, columns)
        out_ref[:, :, columns] = got_ref[:, hours:, columns] - mixed


def residual_of(at, khi, klo, got, other):
    chips, hours, sites = other.shape
    return pl.pallas_call(
        residual_kernel,
        in_specs=[SMEM] + [VMEM] * 4,
        out_specs=VMEM,
        out_shape=jax.ShapeDtypeStruct(other.shape, F32),
        scratch_shapes=[pltpu.VMEM((2 * chips * hours, sites), BF16)] * 2,
        compiler_params=params(24),
        cost_estimate=cost(0, 0),
        name="residual_of",
    )(at, khi, klo, got, other)


def image_kernel(at_ref, khi_ref, klo_ref, own_ref, other_ref, r_ref, noise_ref, out_ref, sums_ref, uhi_ref, ulo_ref, image_ref, sems):
    chips, hours, sites = own_ref.shape
    width = sites // 2
    places = [slice(part * width, (part + 1) * width) for part in range(2)]
    copies = [
        pltpu.make_async_copy(image_ref.at[:, :, place], out_ref.at[:, pl.ds(0, hours), place], sems.at[part])
        for part, place in enumerate(places)
    ]
    kept = pltpu.make_async_copy(r_ref, out_ref.at[:, pl.ds(hours, hours)], sems.at[2])
    kept.start()
    split_hours(at_ref, own_ref, other_ref, uhi_ref, ulo_ref)
    squares = jnp.zeros((8, TILE), F32)
    curves = jnp.zeros((8, TILE), F32)
    for copy, columns in zip(copies, places):
        mixed = time_product(khi_ref, klo_ref, uhi_ref, ulo_ref, columns)
        r = r_ref[:, :, columns]
        image = mixed + noise_ref[:, columns][None] * r
        image_ref[:, :, columns] = image
        copy.start()
        for t in range(width // TILE):
            piece = slice(t * TILE, (t + 1) * TILE)
            a, b = r[:, :, piece].reshape(-1, 8, TILE), image[:, :, piece].reshape(-1, 8, TILE)
            squares += jnp.sum(a * a, axis=0)
            curves += jnp.sum(a * b, axis=0)
    sums_ref[:8, :] = squares
    sums_ref[8:, :] = curves
    for copy in copies + [kept]:
        copy.wait()


def image_of(at, khi, klo, own, other, residual, noise):
    chips, hours, sites = own.shape
    return pl.pallas_call(
        image_kernel,
        in_specs=[SMEM] + [VMEM] * 6,
        out_specs=[ANY, VMEM],
        out_shape=[jax.ShapeDtypeStruct((chips, 2 * hours, sites), F32), jax.ShapeDtypeStruct((16, TILE), F32)],
        scratch_shapes=[pltpu.VMEM((2 * chips * hours, sites), BF16)] * 2
        + [pltpu.VMEM(own.shape, F32), pltpu.SemaphoreType.DMA((3,))],
        compiler_params=params(24),
        cost_estimate=cost(0, 0),
        name="image_of",
    )(at, khi, klo, own, other, residual, noise)


def update_kernel(start_ref, got_ref, *refs):
    sums, (iterate_ref, next_ref) = refs[:-2], refs[-2:]
    chips, _, width = got_ref.shape
    hours = start_ref.shape[0]
    total = sums[0][...]
    for part in sums[1:]:
        total += part[...]
    alpha = jnp.sum(total[:8, :]) / jnp.sum(total[8:, :])
    for g in range(chips):
        columns = slice(g * width, (g + 1) * width)
        r = got_ref[g, hours:, :]
        iterate_ref[:, columns] = start_ref[:, columns] + alpha * r
        next_ref[:, columns] = r - alpha * got_ref[g, :hours, :]


def update(start, got, sums):
    shape = jax.ShapeDtypeStruct(start.shape, F32)
    return pl.pallas_call(
        update_kernel,
        in_specs=[VMEM] * (2 + len(sums)),
        out_specs=(VMEM, VMEM),
        out_shape=(shape, shape),
        compiler_params=params(24),
        cost_estimate=cost(0, 0),
        name="update",
    )(start, got, *sums)


def first_rows_kernel(value_ref, *refs):
    refs[-1][...] = value_ref[:, : refs[-1].shape[1], :]


def first_rows(value, rows, after):
    return pl.pallas_call(
        first_rows_kernel,
        in_specs=[VMEM] + [ANY] * len(after),
        out_specs=VMEM,
        out_shape=jax.ShapeDtypeStruct((value.shape[0], rows, value.shape[2]), F32),
        compiler_params=params(16),
        cost_estimate=cost(0, 0),
        name="first_rows",
    )(value, *after)


def ordered(value, *after):
    return pl.pallas_call(
        lambda *refs: None,
        in_specs=[ANY] * (1 + len(after)),
        out_specs=ANY,
        out_shape=jax.ShapeDtypeStruct(value.shape, value.dtype),
        input_output_aliases={0: 0},
        cost_estimate=cost(0, 0),
        name="ordered",
    )(value, *after)


def joined_kernel(a_ref, b_ref, *refs):
    refs[-1][: a_ref.shape[0]] = a_ref[...]
    refs[-1][a_ref.shape[0] :] = b_ref[...]


def joined(a, b, after):
    return pl.pallas_call(
        joined_kernel,
        in_specs=[VMEM] * 2 + [ANY] * len(after),
        out_specs=VMEM,
        out_shape=jax.ShapeDtypeStruct((a.shape[0] + b.shape[0],) + a.shape[1:], F32),
        compiler_params=params(8),
        cost_estimate=cost(0, 0),
        name="joined",
    )(a, b, *after)


def token(value):
    return value.reshape((-1,) + value.shape[-2:])[0, :16, :TILE]


def exchange(blocks):
    return lax.all_to_all(blocks, "tm", 0, 0, axis_index_groups=SAME_CORE, tiled=True)


def along_side(shift, axis):
    place = lambda a, b: a * SIDE + b
    if axis == "y":
        return [(place(a, b), place(a, (b + shift) % SIDE)) for a in range(SIDE) for b in range(SIDE)]
    return [(place(a, b), place((a + shift) % SIDE, b)) for a in range(SIDE) for b in range(SIDE)]


def local(start, right_side, noise, tile_ids, space_tiles, time_kernel):
    hours_dev, sites_dev = start.shape
    count = tile_ids.shape[0]
    width = sites_dev // CHIPS
    edge = REACH * TILE
    spaces = lax.axis_size("space")
    space, tm = lax.axis_index("space"), lax.axis_index("tm")
    chip, core = tm // 2, tm % 2
    base = space * count - REACH
    at = jnp.stack([chip, core, base + chip * (count // CHIPS), base, space % SIDE]).astype(jnp.int32)

    forward = [(i, i + 1) for i in range(spaces - 1)]
    backward = [(target, source) for source, target in forward]
    low = lax.ppermute(start[:, sites_dev - edge :], "space", forward)
    high = lax.ppermute(start[:, :edge], "space", backward)
    rows = time_kernel.shape[0] // SIDE
    ids = tile_ids.T
    strip = lax.dynamic_slice(time_kernel, (space % SIDE * rows, 0), (rows, time_kernel.shape[1]))[None]
    far = lax.ppermute(strip, "tm", along_z(4))
    strip = joined(strip, far, [token(low), token(high)])
    far = lax.ppermute(strip, "tm", along_z(2))
    sent = space_wide(0, at, ids, low, start, space_tiles, right_side, noise, None, [])
    strip = joined(strip, far, [token(sent)])
    far = lax.ppermute(strip, "tm", along_z(-1))
    sent = space_wide(CHIPS // 2, at, ids, high, start, space_tiles, right_side, noise, sent, [token(strip)])
    strip = joined(strip, far, [])
    strips = [strip] + [lax.ppermute(strip, "space", along_side(-k, "y")) for k in range(1, SIDE)]
    khi, klo = time_rows(at, strips)
    weights = weights_of(at, space_tiles)

    got = exchange(ordered(sent, token(far)))
    other = lax.ppermute(first_rows(got, hours_dev, [token(khi), token(weights)]), "tm", SWAP)
    residual = residual_of(at, khi, klo, got, other)

    up, down = [], []
    for s in range(spaces):
        for z in range(CHIPS):
            for c in range(2):
                source, target = (s * CHIPS + z), (s * CHIPS + z + 1)
                if target < spaces * CHIPS:
                    up.append((source * 2 + c, target * 2 + c))
                    down.append((target * 2 + c, source * 2 + c))
    left = lax.ppermute(residual[:, :, width - edge :], ("space", "tm"), up)
    right = lax.ppermute(residual[:, :, :edge], ("space", "tm"), down)
    mixed = space_mixed(at, ids, left, residual, right, weights, [])
    other = lax.ppermute(mixed, "tm", SWAP)
    noise_here = lax.dynamic_slice(noise, (chip * width,), (width,))[None, :]
    image, sums = image_of(at, khi, klo, mixed, other, residual, noise_here)
    back = exchange(image)
    sums = sums + lax.ppermute(sums, "tm", SWAP)
    for axis in ("y", "x"):
        for shift in (2, 1):
            sums = sums + lax.ppermute(sums, "space", along_side(shift, axis))
    sums = [sums] + [lax.ppermute(sums, "tm", along_z(shift)) for shift in range(1, CHIPS)]
    return update(start, back, sums)


def solution(mesh):
    placed = (
        P("tm", "space"),
        P("tm", "space"),
        P("space"),
        P("space", None),
        P("space", None, None, None),
        P("tm", None),
    )
    return jax.shard_map(
        local,
        mesh=mesh,
        in_specs=placed,
        out_specs=(P("tm", "space"), P("tm", "space")),
        check_vma=False,
    )
```

```python
import jax
import jax.numpy as jnp
from jax import lax
from jax.experimental import pallas as pl
from jax.experimental.pallas import tpu as pltpu
from jax.sharding import PartitionSpec as P

REACH = 2
TILE = 128
CHIPS = 8
SAME_CORE = [[chip * 2 + core for chip in range(CHIPS)] for core in range(2)]
SIDE = 4
ORIGIN = (0, 4, 6, 2, 1, 5, 7, 3)
SWAP = [(i, i ^ 1) for i in range(2 * CHIPS)]
F32 = jnp.float32
BF16 = jnp.bfloat16
VMEM = pl.BlockSpec(memory_space=pltpu.VMEM)
SMEM = pl.BlockSpec(memory_space=pltpu.SMEM)
ANY = pl.BlockSpec(memory_space=pl.ANY)
HBM = pl.BlockSpec(memory_space=pltpu.HBM)


def along_z(shift):
    return [(z * 2 + c, (z + shift) % CHIPS * 2 + c) for z in range(CHIPS) for c in range(2)]


def halves(value):
    high = value.astype(BF16)
    return high, (value - high.astype(F32)).astype(BF16)


def turned(at, index):
    return jnp.where(at[6] == 1, CHIPS - 1 - index, index)


def params(megabytes):
    return pltpu.CompilerParams(vmem_limit_bytes=megabytes * 1024 * 1024)


def cost(flops, moved):
    return pl.CostEstimate(flops=flops, bytes_accessed=moved, transcendentals=0)


def dot_nt(a, b):
    return lax.dot_general(a, b, (((1,), (1,)), ((), ())), preferred_element_type=F32)


def dot_nn(a, b):
    return lax.dot_general(a, b, (((1,), (0,)), ((), ())), preferred_element_type=F32)


def stacked_halves(tiles):
    high, low = halves(tiles)
    return jnp.concatenate([high, low], axis=-2)


def weights_kernel(at_ref, tiles_ref, out_ref):
    out_ref[...] = stacked_halves(tiles_ref[...])


def weights_of(at, tiles):
    count, nb = tiles.shape[:2]
    rows = count // CHIPS
    return pl.pallas_call(
        weights_kernel,
        grid_spec=pltpu.PrefetchScalarGridSpec(
            num_scalar_prefetch=1,
            grid=(rows,),
            in_specs=[pl.BlockSpec((1, nb, TILE, TILE), lambda i, at: (at[5] * rows + i, 0, 0, 0))],
            out_specs=pl.BlockSpec((1, nb, 2 * TILE, TILE), lambda i, at: (i, 0, 0, 0)),
        ),
        out_shape=jax.ShapeDtypeStruct((rows, nb, 2 * TILE, TILE), BF16),
        compiler_params=params(56),
        cost_estimate=cost(0, 0),
        name="weights_of",
    )(at, tiles)


def space_wide_kernel(first, at_ref, ids_ref, edge_ref, noise_ref, x_ref, tiles_ref, right_ref, *refs):
    out_ref, win_ref, x_here, tile_ref, right_here, stage_ref, x_sems, tile_sems, right_sems, out_sems = refs[-10:]
    hours, sites = x_ref.shape
    groups = stage_ref.shape[0]
    rows, nb = tile_ref.shape[0] // groups, tile_ref.shape[1]
    width = rows * TILE
    count = sites // TILE
    needed = range(first * rows, (first + groups) * rows + 2 * REACH)
    inside = [i - REACH for i in needed if 0 <= i - REACH < count]
    pieces = range(inside[0] // rows, inside[-1] // rows + 1)
    place = lambda g: slice(g * width, (g + 1) * width)
    fetch = [pltpu.make_async_copy(x_ref.at[:, place(g)], x_here.at[:, place(g)], x_sems.at[g]) for g in pieces]
    tiles = [
        pltpu.make_async_copy(tiles_ref.at[first * rows + k], tile_ref.at[k], tile_sems.at[k])
        for k in range(rows * groups)
    ]
    right = [
        pltpu.make_async_copy(right_ref.at[:, place(first + k)], right_here.at[k], right_sems.at[k]) for k in range(groups)
    ]
    for copy in fetch + tiles + right:
        copy.start()
    for copy in fetch:
        copy.wait()
    for k, i in enumerate(needed):
        if i < REACH:
            piece = edge_ref[:, i * TILE : (i + 1) * TILE]
        elif i < count + REACH:
            piece = x_here[:, (i - REACH) * TILE : (i - REACH + 1) * TILE]
        else:
            j = i - count - REACH
            piece = edge_ref[:, j * TILE : (j + 1) * TILE]
        high, low = halves(piece)
        win_ref[k, :hours, :] = high
        win_ref[k, hours:, :] = low
    sent = []
    for k in range(groups):
        for i in range(rows):
            tiles[k * rows + i].wait()
        for i in range(rows):
            row = (first + k) * rows + i
            field = [win_ref[ids_ref[n, row] - at_ref[3] - first * rows] for n in range(nb)]
            mine = jnp.concatenate([tile_ref[k * rows + i, n] for n in range(nb)], axis=1)
            product = dot_nt(jnp.concatenate(field, axis=1), stacked_halves(mine))
            columns = slice(i * TILE, (i + 1) * TILE)
            stage_ref[k, :hours, columns] = product[:hours, :TILE] + (product[:hours, TILE:] + product[hours:, :TILE])
        right[k].wait()
        stage_ref[k, hours:, :] = right_here[k] - noise_ref[:, place(first + k)] * x_here[:, place(first + k)]
        sent.append(pltpu.make_async_copy(stage_ref.at[k], out_ref.at[turned(at_ref, first + k)], out_sems.at[k]))
        sent[-1].start()
    for copy in sent:
        copy.wait()


def space_wide(first, at, ids, edge, x, tiles, right_side, noise, begun, after):
    hours, sites = x.shape
    nb, count = ids.shape
    rows, groups = count // CHIPS, CHIPS // 2
    more = ([] if begun is None else [begun]) + after
    return pl.pallas_call(
        lambda *refs: space_wide_kernel(first, *refs),
        in_specs=[SMEM] * 2 + [VMEM] * 2 + [HBM] * 3 + [ANY] * len(more),
        out_specs=ANY,
        out_shape=jax.ShapeDtypeStruct((CHIPS, 2 * hours, rows * TILE), F32),
        input_output_aliases={} if begun is None else {7: 0},
        scratch_shapes=[
            pltpu.VMEM((count // 2 + 2 * REACH, 2 * hours, TILE), BF16),
            pltpu.VMEM((hours, sites), F32),
            pltpu.VMEM((rows * groups, nb, TILE, TILE), F32),
            pltpu.VMEM((groups, hours, rows * TILE), F32),
            pltpu.VMEM((groups, 2 * hours, rows * TILE), F32),
            pltpu.SemaphoreType.DMA((CHIPS,)),
            pltpu.SemaphoreType.DMA((rows * groups,)),
            pltpu.SemaphoreType.DMA((groups,)),
            pltpu.SemaphoreType.DMA((groups,)),
        ],
        compiler_params=params(56),
        cost_estimate=cost(0, 0),
        name="space_wide",
    )(at, ids, edge, noise[None, :], x, tiles, right_side, *more)


def space_mixed_kernel(at_ref, ids_ref, left_ref, own_ref, right_ref, weights_ref, *refs):
    out_ref, hi_ref, lo_ref = refs[-3:]
    rows, nb = weights_ref.shape[:2]
    for i in range(rows + 2 * REACH):
        if i < REACH:
            piece = left_ref[:, :, i * TILE : (i + 1) * TILE]
        elif i < rows + REACH:
            piece = own_ref[:, :, (i - REACH) * TILE : (i - REACH + 1) * TILE]
        else:
            k = i - rows - REACH
            piece = right_ref[:, :, k * TILE : (k + 1) * TILE]
        high, low = halves(piece.reshape(-1, TILE))
        hi_ref[i] = high
        lo_ref[i] = low
    for row in range(rows):
        total = None
        for n in range(nb):
            i = ids_ref[n, at_ref[5] * rows + row] - at_ref[2]
            both = dot_nt(hi_ref[i], weights_ref[row, n])
            part = both[:, :TILE] + (both[:, TILE:] + dot_nt(lo_ref[i], weights_ref[row, n, :TILE]))
            total = part if total is None else total + part
        out_ref[:, :, row * TILE : (row + 1) * TILE] = total.reshape(out_ref.shape[:2] + (TILE,))


def space_mixed(at, ids, left, own, right, weights, after):
    nb, count = ids.shape
    rows, hours = count // CHIPS, own.shape[0] * own.shape[1]
    whole = lambda i, at, ids: (0, 0, 0)
    return pl.pallas_call(
        space_mixed_kernel,
        grid_spec=pltpu.PrefetchScalarGridSpec(
            num_scalar_prefetch=2,
            grid=(1,),
            in_specs=[
                pl.BlockSpec(left.shape, whole),
                pl.BlockSpec(own.shape, whole),
                pl.BlockSpec(right.shape, whole),
                pl.BlockSpec((rows, nb, 2 * TILE, TILE), lambda i, at, ids: (0, 0, 0, 0)),
            ]
            + [ANY] * len(after),
            out_specs=pl.BlockSpec(own.shape, whole),
            scratch_shapes=[pltpu.VMEM((rows + 2 * REACH, hours, TILE), BF16)] * 2,
        ),
        out_shape=jax.ShapeDtypeStruct(own.shape, F32),
        compiler_params=params(24),
        cost_estimate=cost(4000000000, 0),
        name="space_mixed",
    )(at, ids, left, own, right, weights, *after)


def time_rows_kernel(at_ref, *refs):
    strips, (hi_ref, lo_ref) = refs[:SIDE], refs[SIDE:]
    chips, rows, _ = strips[0].shape
    for k in range(SIDE):
        row = pl.multiple_of((at_ref[4] + k) % SIDE * rows, rows)
        for j in range(chips):
            chip = (at_ref[0] + ORIGIN[j]) % chips
            high, low = halves(strips[k][j])
            hi_ref[chip, pl.ds(row, rows), :] = high
            lo_ref[chip, pl.ds(row, rows), :] = low


def time_rows(at, strips):
    chips, rows, depth = strips[0].shape
    shape = jax.ShapeDtypeStruct((chips, rows * SIDE, depth), BF16)
    return pl.pallas_call(
        time_rows_kernel,
        in_specs=[SMEM] + [VMEM] * SIDE,
        out_specs=(VMEM, VMEM),
        out_shape=(shape, shape),
        compiler_params=params(16),
        cost_estimate=cost(0, 0),
        name="time_rows",
    )(at, *strips)


def split_hours(at_ref, own_ref, other_ref, uhi_ref, ulo_ref):
    hours = other_ref.shape[1]
    for chip in range(CHIPS):
        for ref, core in ((own_ref, at_ref[1]), (other_ref, 1 - at_ref[1])):
            row = pl.multiple_of((2 * chip + core) * hours, hours)
            high, low = halves(ref[chip, :hours, :])
            uhi_ref[pl.ds(row, hours), :] = high
            ulo_ref[pl.ds(row, hours), :] = low


def time_product(khi_ref, klo_ref, uhi_ref, ulo_ref, columns):
    chips, hours, depth = khi_ref.shape
    khi = khi_ref[...].reshape(chips * hours, depth)
    klo = klo_ref[...].reshape(chips * hours, depth)
    uhi, ulo = uhi_ref[:, columns], ulo_ref[:, columns]
    mixed = dot_nn(khi, uhi) + (dot_nn(khi, ulo) + dot_nn(klo, uhi))
    return mixed.reshape(chips, hours, -1)


def residual_kernel(at_ref, khi_ref, klo_ref, got_ref, other_ref, out_ref, uhi_ref, ulo_ref):
    chips, hours, sites = out_ref.shape
    split_hours(at_ref, got_ref, other_ref, uhi_ref, ulo_ref)
    width = sites // 2
    for part in range(2):
        columns = slice(part * width, (part + 1) * width)
        mixed = time_product(khi_ref, klo_ref, uhi_ref, ulo_ref, columns)
        out_ref[:, :, columns] = got_ref[:, hours:, columns] - mixed


def residual_of(at, khi, klo, got, other):
    chips, hours, sites = other.shape
    return pl.pallas_call(
        residual_kernel,
        in_specs=[SMEM] + [VMEM] * 4,
        out_specs=VMEM,
        out_shape=jax.ShapeDtypeStruct(other.shape, F32),
        scratch_shapes=[pltpu.VMEM((2 * chips * hours, sites), BF16)] * 2,
        compiler_params=params(24),
        cost_estimate=cost(0, 0),
        name="residual_of",
    )(at, khi, klo, got, other)


def image_kernel(at_ref, khi_ref, klo_ref, own_ref, other_ref, r_ref, noise_ref, out_ref, sums_ref, uhi_ref, ulo_ref):
    chips, hours, sites = own_ref.shape
    split_hours(at_ref, own_ref, other_ref, uhi_ref, ulo_ref)
    width = sites // 2
    squares = jnp.zeros((8, TILE), F32)
    curves = jnp.zeros((8, TILE), F32)
    for part in range(2):
        columns = slice(part * width, (part + 1) * width)
        mixed = time_product(khi_ref, klo_ref, uhi_ref, ulo_ref, columns)
        r = r_ref[:, :, columns]
        image = mixed + noise_ref[:, columns][None] * r
        out_ref[:, :, columns] = image
        for t in range(width // TILE):
            piece = slice(t * TILE, (t + 1) * TILE)
            a, b = r[:, :, piece].reshape(-1, 8, TILE), image[:, :, piece].reshape(-1, 8, TILE)
            squares += jnp.sum(a * a, axis=0)
            curves += jnp.sum(a * b, axis=0)
    sums_ref[:8, :] = squares
    sums_ref[8:, :] = curves


def image_of(at, khi, klo, own, other, residual, noise):
    chips, hours, sites = own.shape
    return pl.pallas_call(
        image_kernel,
        in_specs=[SMEM] + [VMEM] * 6,
        out_specs=[VMEM] * 2,
        out_shape=[jax.ShapeDtypeStruct(own.shape, F32), jax.ShapeDtypeStruct((16, TILE), F32)],
        scratch_shapes=[pltpu.VMEM((2 * chips * hours, sites), BF16)] * 2,
        compiler_params=params(24),
        cost_estimate=cost(0, 0),
        name="image_of",
    )(at, khi, klo, own, other, residual, noise)


def update_kernel(at_ref, start_ref, residual_ref, image_ref, *refs):
    sums, (iterate_ref, next_ref) = refs[:-2], refs[-2:]
    chips, _, width = residual_ref.shape
    total = sums[0][...]
    for part in sums[1:]:
        total += part[...]
    alpha = jnp.sum(total[:8, :]) / jnp.sum(total[8:, :])
    for g in range(chips):
        columns = slice(g * width, (g + 1) * width)
        chip = turned(at_ref, g)
        r = residual_ref[chip]
        iterate_ref[:, columns] = start_ref[:, columns] + alpha * r
        next_ref[:, columns] = r - alpha * image_ref[chip]


def update(at, start, residual, image, sums):
    shape = jax.ShapeDtypeStruct(start.shape, F32)
    return pl.pallas_call(
        update_kernel,
        in_specs=[SMEM] + [VMEM] * (3 + len(sums)),
        out_specs=(VMEM, VMEM),
        out_shape=(shape, shape),
        compiler_params=params(24),
        cost_estimate=cost(0, 0),
        name="update",
    )(at, start, residual, image, *sums)


def first_rows_kernel(value_ref, *refs):
    refs[-1][...] = value_ref[:, : refs[-1].shape[1], :]


def first_rows(value, rows, after):
    return pl.pallas_call(
        first_rows_kernel,
        in_specs=[VMEM] + [ANY] * len(after),
        out_specs=VMEM,
        out_shape=jax.ShapeDtypeStruct((value.shape[0], rows, value.shape[2]), F32),
        compiler_params=params(16),
        cost_estimate=cost(0, 0),
        name="first_rows",
    )(value, *after)


def ordered(value, *after):
    return pl.pallas_call(
        lambda *refs: None,
        in_specs=[ANY] * (1 + len(after)),
        out_specs=ANY,
        out_shape=jax.ShapeDtypeStruct(value.shape, value.dtype),
        input_output_aliases={0: 0},
        cost_estimate=cost(0, 0),
        name="ordered",
    )(value, *after)


def joined_kernel(a_ref, b_ref, *refs):
    refs[-1][: a_ref.shape[0]] = a_ref[...]
    refs[-1][a_ref.shape[0] :] = b_ref[...]


def joined(a, b, after):
    return pl.pallas_call(
        joined_kernel,
        in_specs=[VMEM] * 2 + [ANY] * len(after),
        out_specs=VMEM,
        out_shape=jax.ShapeDtypeStruct((a.shape[0] + b.shape[0],) + a.shape[1:], F32),
        compiler_params=params(8),
        cost_estimate=cost(0, 0),
        name="joined",
    )(a, b, *after)


def copied_kernel(value_ref, out_ref, sem):
    copy = pltpu.make_async_copy(value_ref, out_ref, sem)
    copy.start()
    copy.wait()


def copied(value):
    return pl.pallas_call(
        copied_kernel,
        in_specs=[VMEM],
        out_specs=ANY,
        out_shape=jax.ShapeDtypeStruct(value.shape, value.dtype),
        scratch_shapes=[pltpu.SemaphoreType.DMA],
        compiler_params=params(16),
        cost_estimate=cost(0, 0),
        name="copied",
    )(value)


def token(value):
    return value.reshape((-1,) + value.shape[-2:])[0, :16, :TILE]


def exchange(blocks):
    return lax.all_to_all(blocks, "tm", 0, 0, axis_index_groups=SAME_CORE, tiled=True)


def along_side(shift, axis):
    place = lambda a, b: a * SIDE + b
    if axis == "y":
        return [(place(a, b), place(a, (b + shift) % SIDE)) for a in range(SIDE) for b in range(SIDE)]
    return [(place(a, b), place((a + shift) % SIDE, b)) for a in range(SIDE) for b in range(SIDE)]


def local(start, right_side, noise, tile_ids, space_tiles, time_kernel):
    hours_dev, sites_dev = start.shape
    count = tile_ids.shape[0]
    width = sites_dev // CHIPS
    edge = REACH * TILE
    spaces = lax.axis_size("space")
    space, tm = lax.axis_index("space"), lax.axis_index("tm")
    chip, core = tm // 2, tm % 2
    base = space * count - REACH
    flip = space % 2
    group = jnp.where(flip == 1, CHIPS - 1 - chip, chip)
    at = jnp.stack([chip, core, base + group * (count // CHIPS), base, space % SIDE, group, flip]).astype(jnp.int32)

    forward = [(i, i + 1) for i in range(spaces - 1)]
    backward = [(target, source) for source, target in forward]
    low = lax.ppermute(start[:, sites_dev - edge :], "space", forward)
    high = lax.ppermute(start[:, :edge], "space", backward)
    rows = time_kernel.shape[0] // SIDE
    ids = tile_ids.T
    strip = lax.dynamic_slice(time_kernel, (space % SIDE * rows, 0), (rows, time_kernel.shape[1]))[None]
    far = lax.ppermute(strip, "tm", along_z(4))
    strip = joined(strip, far, [token(low), token(high)])
    far = lax.ppermute(strip, "tm", along_z(2))
    sent = space_wide(0, at, ids, low, start, space_tiles, right_side, noise, None, [])
    strip = joined(strip, far, [token(sent)])
    far = lax.ppermute(strip, "tm", along_z(-1))
    sent = space_wide(CHIPS // 2, at, ids, high, start, space_tiles, right_side, noise, sent, [token(strip)])
    strip = joined(strip, far, [])
    strips = [strip] + [lax.ppermute(strip, "space", along_side(-k, "y")) for k in range(1, SIDE)]
    khi, klo = time_rows(at, strips)
    weights = weights_of(at, space_tiles)

    got = exchange(ordered(sent, token(far)))
    other = lax.ppermute(first_rows(got, hours_dev, [token(khi), token(weights)]), "tm", SWAP)
    residual = residual_of(at, khi, klo, got, other)

    up, down = [], []
    line = [s * CHIPS + (CHIPS - 1 - g if s % 2 else g) for s in range(spaces) for g in range(CHIPS)]
    for source, target in zip(line, line[1:]):
        for c in range(2):
            up.append((source * 2 + c, target * 2 + c))
            down.append((target * 2 + c, source * 2 + c))
    left = lax.ppermute(residual[:, :, width - edge :], ("space", "tm"), up)
    right = lax.ppermute(residual[:, :, :edge], ("space", "tm"), down)
    back_r = exchange(copied(residual))
    mixed = space_mixed(at, ids, left, residual, right, weights, [])
    other = lax.ppermute(mixed, "tm", SWAP)
    noise_here = lax.dynamic_slice(noise, (group * width,), (width,))[None, :]
    image, sums = image_of(at, khi, klo, mixed, other, residual, noise_here)
    sums = sums + lax.ppermute(sums, "tm", SWAP)
    sums = sums + lax.ppermute(sums, "tm", along_z(CHIPS // 2))
    back_p = exchange(ordered(image, sums))
    for axis in ("y", "x"):
        sums = sum([lax.ppermute(sums, "space", along_side(shift, axis)) for shift in range(1, SIDE)], sums)
    sums = [sums] + [lax.ppermute(sums, "tm", along_z(shift)) for shift in range(1, CHIPS // 2)]
    return update(at, start, back_r, back_p, sums)


def solution(mesh):
    placed = (
        P("tm", "space"),
        P("tm", "space"),
        P("space"),
        P("space", None),
        P("space", None, None, None),
        P("tm", None),
    )
    return jax.shard_map(
        local,
        mesh=mesh,
        in_specs=placed,
        out_specs=(P("tm", "space"), P("tm", "space")),
        check_vma=False,
    )
```

```python
import jax
import jax.numpy as jnp
from jax import lax
from jax.experimental import pallas as pl
from jax.experimental.pallas import tpu as pltpu
from jax.sharding import PartitionSpec as P

REACH = 2
TILE = 128
CHIPS = 8
SAME_CORE = [[chip * 2 + core for chip in range(CHIPS)] for core in range(2)]
SIDE = 4
ORIGIN = (0, 4, 1, 5, 7, 3, 6, 2)
SWAP = [(i, i ^ 1) for i in range(2 * CHIPS)]
F32 = jnp.float32
BF16 = jnp.bfloat16
VMEM = pl.BlockSpec(memory_space=pltpu.VMEM)
SMEM = pl.BlockSpec(memory_space=pltpu.SMEM)
ANY = pl.BlockSpec(memory_space=pl.ANY)
HBM = pl.BlockSpec(memory_space=pltpu.HBM)


def along_z(shift):
    return [(z * 2 + c, (z + shift) % CHIPS * 2 + c) for z in range(CHIPS) for c in range(2)]


def halves(value):
    high = value.astype(BF16)
    return high, (value - high.astype(F32)).astype(BF16)


def turned(space, index):
    return jnp.where(space % 2 == 1, CHIPS - 1 - index, index)


def params(megabytes):
    return pltpu.CompilerParams(vmem_limit_bytes=megabytes * 1024 * 1024)


def cost(flops, moved):
    return pl.CostEstimate(flops=flops, bytes_accessed=moved, transcendentals=0)


def dot_nt(a, b):
    return lax.dot_general(a, b, (((1,), (1,)), ((), ())), preferred_element_type=F32)


def dot_nn(a, b):
    return lax.dot_general(a, b, (((1,), (0,)), ((), ())), preferred_element_type=F32)


def stacked_halves(tiles):
    high, low = halves(tiles)
    return jnp.concatenate([high, low], axis=-2)


def weights_kernel(at_ref, tiles_ref, out_ref):
    out_ref[...] = stacked_halves(tiles_ref[...])


def weights_of(at, tiles):
    count, nb = tiles.shape[:2]
    rows = count // CHIPS
    return pl.pallas_call(
        weights_kernel,
        grid_spec=pltpu.PrefetchScalarGridSpec(
            num_scalar_prefetch=1,
            grid=(rows,),
            in_specs=[pl.BlockSpec((1, nb, TILE, TILE), lambda i, at: (at[5] * rows + i, 0, 0, 0))],
            out_specs=pl.BlockSpec((1, nb, 2 * TILE, TILE), lambda i, at: (i, 0, 0, 0)),
        ),
        out_shape=jax.ShapeDtypeStruct((rows, nb, 2 * TILE, TILE), BF16),
        compiler_params=params(56),
        cost_estimate=cost(0, 0),
        name="weights_of",
    )(at, tiles)


def space_wide_kernel(ids_ref, low_ref, high_ref, noise_ref, x_ref, tiles_ref, right_ref, *refs):
    out_ref, win_ref, x_here, tile_ref, right_here, stage_ref, sems, out_sems = refs
    hours, sites = x_ref.shape
    space = lax.axis_index("space")
    groups = stage_ref.shape[0]
    rows, nb = tile_ref.shape[0] // groups, tile_ref.shape[1]
    width = rows * TILE
    count = sites // TILE
    base = space * count - REACH
    place = lambda g: slice(g * width, (g + 1) * width)
    x_copy = pltpu.make_async_copy(x_ref, x_here, sems.at[groups])
    right_copy = pltpu.make_async_copy(right_ref, right_here, sems.at[groups + 1])
    tiles = [
        pltpu.make_async_copy(tiles_ref.at[pl.ds(g * rows, rows)], tile_ref.at[pl.ds(g * rows, rows)], sems.at[g])
        for g in range(groups)
    ]
    x_copy.start()
    tiles[0].start()
    right_copy.start()
    for copy in tiles[1:]:
        copy.start()

    def keep(i, piece):
        high, low = halves(piece)
        win_ref[i, :hours, :] = high
        win_ref[i, hours:, :] = low

    for i in range(REACH):
        keep(i, low_ref[:, i * TILE : (i + 1) * TILE])
        keep(i + count + REACH, high_ref[:, i * TILE : (i + 1) * TILE])
    x_copy.wait()
    for i in range(count):
        keep(i + REACH, x_here[:, i * TILE : (i + 1) * TILE])
    sent = []
    for g in range(groups):
        tiles[g].wait()
        for i in range(rows):
            row = g * rows + i
            field = [win_ref[ids_ref[n, row] - base] for n in range(nb)]
            mine = jnp.concatenate([tile_ref[row, n] for n in range(nb)], axis=1)
            product = dot_nt(jnp.concatenate(field, axis=1), stacked_halves(mine))
            columns = slice(i * TILE, (i + 1) * TILE)
            stage_ref[g, :hours, columns] = product[:hours, :TILE] + (product[:hours, TILE:] + product[hours:, :TILE])
        if g == 0:
            right_copy.wait()
        stage_ref[g, hours:, :] = right_here[:, place(g)] - noise_ref[:, place(g)] * x_here[:, place(g)]
        sent.append(pltpu.make_async_copy(stage_ref.at[g], out_ref.at[turned(space, g)], out_sems.at[g]))
        sent[-1].start()
    for copy in sent:
        copy.wait()


def space_wide(ids, low, high, x, tiles, right_side, noise):
    hours, sites = x.shape
    nb, count = ids.shape
    rows = count // CHIPS
    return pl.pallas_call(
        space_wide_kernel,
        in_specs=[SMEM] + [VMEM] * 3 + [HBM] * 3,
        out_specs=ANY,
        out_shape=jax.ShapeDtypeStruct((CHIPS, 2 * hours, rows * TILE), F32),
        scratch_shapes=[
            pltpu.VMEM((count + 2 * REACH, 2 * hours, TILE), BF16),
            pltpu.VMEM((hours, sites), F32),
            pltpu.VMEM((count, nb, TILE, TILE), F32),
            pltpu.VMEM((hours, sites), F32),
            pltpu.VMEM((CHIPS, 2 * hours, rows * TILE), F32),
            pltpu.SemaphoreType.DMA((CHIPS + 2,)),
            pltpu.SemaphoreType.DMA((CHIPS,)),
        ],
        compiler_params=params(56),
        cost_estimate=cost(2 * 10**9, 0),
        name="space_wide",
    )(ids, low, high, noise[None, :], x, tiles, right_side)


def space_mixed_kernel(at_ref, ids_ref, left_ref, own_ref, right_ref, weights_ref, *refs):
    out_ref, hi_ref, lo_ref = refs[-3:]
    rows, nb = weights_ref.shape[:2]
    for i in range(rows + 2 * REACH):
        if i < REACH:
            piece = left_ref[:, :, i * TILE : (i + 1) * TILE]
        elif i < rows + REACH:
            piece = own_ref[:, :, (i - REACH) * TILE : (i - REACH + 1) * TILE]
        else:
            k = i - rows - REACH
            piece = right_ref[:, :, k * TILE : (k + 1) * TILE]
        high, low = halves(piece.reshape(-1, TILE))
        hi_ref[i] = high
        lo_ref[i] = low
    for row in range(rows):
        total = None
        for n in range(nb):
            i = ids_ref[n, at_ref[5] * rows + row] - at_ref[2]
            both = dot_nt(hi_ref[i], weights_ref[row, n])
            part = both[:, :TILE] + (both[:, TILE:] + dot_nt(lo_ref[i], weights_ref[row, n, :TILE]))
            total = part if total is None else total + part
        out_ref[:, :, row * TILE : (row + 1) * TILE] = total.reshape(out_ref.shape[:2] + (TILE,))


def space_mixed(at, ids, left, own, right, weights, after):
    nb, count = ids.shape
    rows, hours = count // CHIPS, own.shape[0] * own.shape[1]
    whole = lambda i, at, ids: (0, 0, 0)
    return pl.pallas_call(
        space_mixed_kernel,
        grid_spec=pltpu.PrefetchScalarGridSpec(
            num_scalar_prefetch=2,
            grid=(1,),
            in_specs=[
                pl.BlockSpec(left.shape, whole),
                pl.BlockSpec(own.shape, whole),
                pl.BlockSpec(right.shape, whole),
                pl.BlockSpec((rows, nb, 2 * TILE, TILE), lambda i, at, ids: (0, 0, 0, 0)),
            ]
            + [ANY] * len(after),
            out_specs=pl.BlockSpec(own.shape, whole),
            scratch_shapes=[pltpu.VMEM((rows + 2 * REACH, hours, TILE), BF16)] * 2,
        ),
        out_shape=jax.ShapeDtypeStruct(own.shape, F32),
        compiler_params=params(24),
        cost_estimate=cost(4000000000, 0),
        name="space_mixed",
    )(at, ids, left, own, right, weights, *after)


def time_rows_kernel(at_ref, *refs):
    strips, (hi_ref, lo_ref) = refs[:SIDE], refs[SIDE:]
    chips, rows, _ = strips[0].shape
    for k in range(SIDE):
        row = pl.multiple_of((at_ref[4] + k) % SIDE * rows, rows)
        for j in range(chips):
            chip = (at_ref[0] + ORIGIN[j]) % chips
            high, low = halves(strips[k][j])
            hi_ref[chip, pl.ds(row, rows), :] = high
            lo_ref[chip, pl.ds(row, rows), :] = low


def time_rows(at, strips):
    chips, rows, depth = strips[0].shape
    shape = jax.ShapeDtypeStruct((chips, rows * SIDE, depth), BF16)
    return pl.pallas_call(
        time_rows_kernel,
        in_specs=[SMEM] + [VMEM] * SIDE,
        out_specs=(VMEM, VMEM),
        out_shape=(shape, shape),
        compiler_params=params(16),
        cost_estimate=cost(0, 0),
        name="time_rows",
    )(at, *strips)


def split_hours(at_ref, own_ref, other_ref, uhi_ref, ulo_ref):
    hours = other_ref.shape[1]
    for chip in range(CHIPS):
        for ref, core in ((own_ref, at_ref[1]), (other_ref, 1 - at_ref[1])):
            row = pl.multiple_of((2 * chip + core) * hours, hours)
            high, low = halves(ref[chip, :hours, :])
            uhi_ref[pl.ds(row, hours), :] = high
            ulo_ref[pl.ds(row, hours), :] = low


def time_product(khi_ref, klo_ref, uhi_ref, ulo_ref, columns):
    chips, hours, depth = khi_ref.shape
    khi = khi_ref[...].reshape(chips * hours, depth)
    klo = klo_ref[...].reshape(chips * hours, depth)
    uhi, ulo = uhi_ref[:, columns], ulo_ref[:, columns]
    mixed = dot_nn(khi, uhi) + (dot_nn(khi, ulo) + dot_nn(klo, uhi))
    return mixed.reshape(chips, hours, -1)


def residual_kernel(at_ref, khi_ref, klo_ref, got_ref, other_ref, out_ref, uhi_ref, ulo_ref):
    chips, hours, sites = out_ref.shape
    split_hours(at_ref, got_ref, other_ref, uhi_ref, ulo_ref)
    width = sites // 2
    for part in range(2):
        columns = slice(part * width, (part + 1) * width)
        mixed = time_product(khi_ref, klo_ref, uhi_ref, ulo_ref, columns)
        out_ref[:, :, columns] = got_ref[:, hours:, columns] - mixed


def residual_of(at, khi, klo, got, other):
    chips, hours, sites = other.shape
    return pl.pallas_call(
        residual_kernel,
        in_specs=[SMEM] + [VMEM] * 4,
        out_specs=VMEM,
        out_shape=jax.ShapeDtypeStruct(other.shape, F32),
        scratch_shapes=[pltpu.VMEM((2 * chips * hours, sites), BF16)] * 2,
        compiler_params=params(24),
        cost_estimate=cost(0, 0),
        name="residual_of",
    )(at, khi, klo, got, other)


def image_kernel(at_ref, khi_ref, klo_ref, own_ref, other_ref, r_ref, noise_ref, out_ref, sums_ref, uhi_ref, ulo_ref):
    chips, hours, sites = own_ref.shape
    split_hours(at_ref, own_ref, other_ref, uhi_ref, ulo_ref)
    width = sites // 2
    squares = jnp.zeros((8, TILE), F32)
    curves = jnp.zeros((8, TILE), F32)
    for part in range(2):
        columns = slice(part * width, (part + 1) * width)
        mixed = time_product(khi_ref, klo_ref, uhi_ref, ulo_ref, columns)
        r = r_ref[:, :, columns]
        image = mixed + noise_ref[:, columns][None] * r
        out_ref[:, :, columns] = image
        for t in range(width // TILE):
            piece = slice(t * TILE, (t + 1) * TILE)
            a, b = r[:, :, piece].reshape(-1, 8, TILE), image[:, :, piece].reshape(-1, 8, TILE)
            squares += jnp.sum(a * a, axis=0)
            curves += jnp.sum(a * b, axis=0)
    sums_ref[:8, :] = squares
    sums_ref[8:, :] = curves


def image_of(at, khi, klo, own, other, residual, noise):
    chips, hours, sites = own.shape
    return pl.pallas_call(
        image_kernel,
        in_specs=[SMEM] + [VMEM] * 6,
        out_specs=[VMEM] * 2,
        out_shape=[jax.ShapeDtypeStruct(own.shape, F32), jax.ShapeDtypeStruct((16, TILE), F32)],
        scratch_shapes=[pltpu.VMEM((2 * chips * hours, sites), BF16)] * 2,
        compiler_params=params(24),
        cost_estimate=cost(0, 0),
        name="image_of",
    )(at, khi, klo, own, other, residual, noise)


def update_kernel(at_ref, start_ref, residual_ref, image_ref, *refs):
    sums, (iterate_ref, next_ref) = refs[:-2], refs[-2:]
    chips, _, width = residual_ref.shape
    total = sums[0][...]
    for part in sums[1:]:
        total += part[...]
    alpha = jnp.sum(total[:8, :]) / jnp.sum(total[8:, :])
    for g in range(chips):
        columns = slice(g * width, (g + 1) * width)
        chip = turned(at_ref[6], g)
        r = residual_ref[chip]
        iterate_ref[:, columns] = start_ref[:, columns] + alpha * r
        next_ref[:, columns] = r - alpha * image_ref[chip]


def update(at, start, residual, image, sums):
    shape = jax.ShapeDtypeStruct(start.shape, F32)
    return pl.pallas_call(
        update_kernel,
        in_specs=[SMEM] + [VMEM] * (3 + len(sums)),
        out_specs=(VMEM, VMEM),
        out_shape=(shape, shape),
        compiler_params=params(24),
        cost_estimate=cost(0, 0),
        name="update",
    )(at, start, residual, image, *sums)


def first_rows_kernel(value_ref, *refs):
    refs[-1][...] = value_ref[:, : refs[-1].shape[1], :]


def first_rows(value, rows, after):
    return pl.pallas_call(
        first_rows_kernel,
        in_specs=[VMEM] + [ANY] * len(after),
        out_specs=VMEM,
        out_shape=jax.ShapeDtypeStruct((value.shape[0], rows, value.shape[2]), F32),
        compiler_params=params(16),
        cost_estimate=cost(0, 0),
        name="first_rows",
    )(value, *after)


def ordered(value, *after):
    return pl.pallas_call(
        lambda *refs: None,
        in_specs=[ANY] + [VMEM] * len(after),
        out_specs=ANY,
        out_shape=jax.ShapeDtypeStruct(value.shape, value.dtype),
        input_output_aliases={0: 0},
        cost_estimate=cost(0, 0),
        name="ordered",
    )(value, *after)


def joined(arrays, after):
    def kernel(*refs):
        first = 0
        for ref in refs[: len(arrays)]:
            refs[-1][first : first + ref.shape[0]] = ref[...]
            first += ref.shape[0]

    return pl.pallas_call(
        kernel,
        in_specs=[VMEM] * (len(arrays) + len(after)),
        out_specs=VMEM,
        out_shape=jax.ShapeDtypeStruct((sum(a.shape[0] for a in arrays),) + arrays[0].shape[1:], F32),
        compiler_params=params(8),
        cost_estimate=cost(0, 0),
        name="joined",
    )(*arrays, *after)


def copied_kernel(value_ref, out_ref, sem):
    copy = pltpu.make_async_copy(value_ref, out_ref, sem)
    copy.start()
    copy.wait()


def copied(value):
    return pl.pallas_call(
        copied_kernel,
        in_specs=[VMEM],
        out_specs=ANY,
        out_shape=jax.ShapeDtypeStruct(value.shape, value.dtype),
        scratch_shapes=[pltpu.SemaphoreType.DMA],
        compiler_params=params(16),
        cost_estimate=cost(0, 0),
        name="copied",
    )(value)


def token(value):
    return value.reshape((-1,) + value.shape[-2:])[0, :16, :TILE]


def exchange(blocks):
    return lax.all_to_all(blocks, "tm", 0, 0, axis_index_groups=SAME_CORE, tiled=True)


def along_side(shift, axis):
    place = lambda a, b: a * SIDE + b
    if axis == "y":
        return [(place(a, b), place(a, (b + shift) % SIDE)) for a in range(SIDE) for b in range(SIDE)]
    return [(place(a, b), place((a + shift) % SIDE, b)) for a in range(SIDE) for b in range(SIDE)]


def local(start, right_side, noise, tile_ids, space_tiles, time_kernel):
    hours_dev, sites_dev = start.shape
    count = tile_ids.shape[0]
    width = sites_dev // CHIPS
    edge = REACH * TILE
    spaces = lax.axis_size("space")
    space, tm = lax.axis_index("space"), lax.axis_index("tm")
    chip, core = tm // 2, tm % 2
    base = space * count - REACH
    group = turned(space, chip)
    at = jnp.stack([chip, core, base + group * (count // CHIPS), base, space % SIDE, group, space]).astype(jnp.int32)

    forward = [(i, i + 1) for i in range(spaces - 1)]
    backward = [(target, source) for source, target in forward]
    low = lax.ppermute(start[:, sites_dev - edge :], "space", forward)
    high = lax.ppermute(start[:, :edge], "space", backward)
    rows = time_kernel.shape[0] // SIDE
    ids = tile_ids.T
    strip = lax.dynamic_slice(time_kernel, (space % SIDE * rows, 0), (rows, time_kernel.shape[1]))[None]
    strip = joined([strip, lax.ppermute(strip, "tm", along_z(CHIPS // 2))], [])
    beside = [lax.ppermute(strip, "tm", along_z(shift)) for shift in (-1, 1, 2)]
    sent = space_wide(ids, low, high, start, space_tiles, right_side, noise)
    strip = joined([strip] + beside, [])
    strips = [strip] + [lax.ppermute(strip, "space", along_side(-k, "y")) for k in range(1, SIDE)]
    khi, klo = time_rows(at, strips)
    weights = weights_of(at, space_tiles)

    got = exchange(ordered(sent, sum(token(b) for b in beside)))
    other = lax.ppermute(first_rows(got, hours_dev, [token(khi), token(weights)]), "tm", SWAP)
    residual = residual_of(at, khi, klo, got, other)

    up, down = [], []
    line = [s * CHIPS + (CHIPS - 1 - g if s % 2 else g) for s in range(spaces) for g in range(CHIPS)]
    for source, target in zip(line, line[1:]):
        for c in range(2):
            up.append((source * 2 + c, target * 2 + c))
            down.append((target * 2 + c, source * 2 + c))
    left = lax.ppermute(residual[:, :, width - edge :], ("space", "tm"), up)
    right = lax.ppermute(residual[:, :, :edge], ("space", "tm"), down)
    back_r = exchange(copied(residual))
    mixed = space_mixed(at, ids, left, residual, right, weights, [])
    other = lax.ppermute(mixed, "tm", SWAP)
    noise_here = lax.dynamic_slice(noise, (group * width,), (width,))[None, :]
    image, sums = image_of(at, khi, klo, mixed, other, residual, noise_here)
    sums = sums + lax.ppermute(sums, "tm", SWAP)
    sums = sums + lax.ppermute(sums, "tm", along_z(CHIPS // 2))
    back_p = exchange(ordered(image, sums))
    for axis in ("y", "x"):
        sums = sum([lax.ppermute(sums, "space", along_side(shift, axis)) for shift in range(1, SIDE)], sums)
    sums = [sums] + [lax.ppermute(sums, "tm", along_z(shift)) for shift in range(1, CHIPS // 2)]
    return update(at, start, back_r, back_p, sums)


def solution(mesh):
    placed = (
        P("tm", "space"),
        P("tm", "space"),
        P("space"),
        P("space", None),
        P("space", None, None, None),
        P("tm", None),
    )
    return jax.shard_map(
        local,
        mesh=mesh,
        in_specs=placed,
        out_specs=(P("tm", "space"), P("tm", "space")),
        check_vma=False,
    )
```

```python
import jax
import jax.numpy as jnp
from jax import lax
from jax.experimental import pallas as pl
from jax.experimental.pallas import tpu as pltpu
from jax.sharding import PartitionSpec as P

REACH = 2
TILE = 128
CHIPS = 8
SAME_CORE = [[chip * 2 + core for chip in range(CHIPS)] for core in range(2)]
SIDE = 4
ORIGIN = (0, 4, 1, 5, 7, 3, 6, 2)
SWAP = [(i, i ^ 1) for i in range(2 * CHIPS)]
F32 = jnp.float32
BF16 = jnp.bfloat16
VMEM = pl.BlockSpec(memory_space=pltpu.VMEM)
SMEM = pl.BlockSpec(memory_space=pltpu.SMEM)
ANY = pl.BlockSpec(memory_space=pl.ANY)
HBM = pl.BlockSpec(memory_space=pltpu.HBM)


def along_z(shift):
    return [(z * 2 + c, (z + shift) % CHIPS * 2 + c) for z in range(CHIPS) for c in range(2)]


def halves(value):
    high = value.astype(BF16)
    return high, (value - high.astype(F32)).astype(BF16)


def turned(space, index):
    return jnp.where(space % 2 == 1, CHIPS - 1 - index, index)


def params(megabytes):
    return pltpu.CompilerParams(vmem_limit_bytes=megabytes * 1024 * 1024)


def cost(flops, moved):
    return pl.CostEstimate(flops=flops, bytes_accessed=moved, transcendentals=0)


def dot_nt(a, b):
    return lax.dot_general(a, b, (((1,), (1,)), ((), ())), preferred_element_type=F32)


def dot_nn(a, b):
    return lax.dot_general(a, b, (((1,), (0,)), ((), ())), preferred_element_type=F32)


def stacked_halves(tiles):
    high, low = halves(tiles)
    return jnp.concatenate([high, low], axis=-2)


def weights_kernel(at_ref, tiles_ref, out_ref):
    out_ref[...] = stacked_halves(tiles_ref[...])


def weights_of(at, tiles):
    count, nb = tiles.shape[:2]
    rows = count // CHIPS
    return pl.pallas_call(
        weights_kernel,
        grid_spec=pltpu.PrefetchScalarGridSpec(
            num_scalar_prefetch=1,
            grid=(rows,),
            in_specs=[pl.BlockSpec((1, nb, TILE, TILE), lambda i, at: (at[5] * rows + i, 0, 0, 0))],
            out_specs=pl.BlockSpec((1, nb, 2 * TILE, TILE), lambda i, at: (i, 0, 0, 0)),
        ),
        out_shape=jax.ShapeDtypeStruct((rows, nb, 2 * TILE, TILE), BF16),
        compiler_params=params(56),
        cost_estimate=cost(0, 0),
        name="weights_of",
    )(at, tiles)


def space_wide_kernel(ids_ref, low_ref, high_ref, noise_ref, x_ref, tiles_ref, right_ref, *refs):
    out_ref, win_ref, x_here, tile_ref, right_here, stage_ref, sems, out_sems = refs
    hours, sites = x_ref.shape
    space = lax.axis_index("space")
    groups = stage_ref.shape[0]
    rows, nb = tile_ref.shape[0] // groups, tile_ref.shape[1]
    width = rows * TILE
    count = sites // TILE
    base = space * count - REACH
    place = lambda g: slice(g * width, (g + 1) * width)
    x_copy = pltpu.make_async_copy(x_ref, x_here, sems.at[groups])
    right_copy = pltpu.make_async_copy(right_ref, right_here, sems.at[groups + 1])
    tiles = [
        pltpu.make_async_copy(tiles_ref.at[pl.ds(g * rows, rows)], tile_ref.at[pl.ds(g * rows, rows)], sems.at[g])
        for g in range(groups)
    ]
    x_copy.start()
    tiles[0].start()
    right_copy.start()
    for copy in tiles[1:]:
        copy.start()

    def keep(i, piece):
        high, low = halves(piece)
        win_ref[i, :hours, :] = high
        win_ref[i, hours:, :] = low

    for i in range(REACH):
        keep(i, low_ref[:, i * TILE : (i + 1) * TILE])
        keep(i + count + REACH, high_ref[:, i * TILE : (i + 1) * TILE])
    x_copy.wait()
    for i in range(count):
        keep(i + REACH, x_here[:, i * TILE : (i + 1) * TILE])
    sent = []
    for g in range(groups):
        tiles[g].wait()
        for i in range(rows):
            row = g * rows + i
            field = [win_ref[ids_ref[n, row] - base] for n in range(nb)]
            mine = jnp.concatenate([tile_ref[row, n] for n in range(nb)], axis=1)
            product = dot_nt(jnp.concatenate(field, axis=1), stacked_halves(mine))
            columns = slice(i * TILE, (i + 1) * TILE)
            stage_ref[g, :hours, columns] = product[:hours, :TILE] + (product[:hours, TILE:] + product[hours:, :TILE])
        if g == 0:
            right_copy.wait()
        stage_ref[g, hours:, :] = right_here[:, place(g)] - noise_ref[:, place(g)] * x_here[:, place(g)]
        sent.append(pltpu.make_async_copy(stage_ref.at[g], out_ref.at[turned(space, g)], out_sems.at[g]))
        sent[-1].start()
    for copy in sent:
        copy.wait()


def space_wide(ids, low, high, x, tiles, right_side, noise):
    hours, sites = x.shape
    nb, count = ids.shape
    rows = count // CHIPS
    return pl.pallas_call(
        space_wide_kernel,
        in_specs=[SMEM] + [VMEM] * 3 + [HBM] * 3,
        out_specs=ANY,
        out_shape=jax.ShapeDtypeStruct((CHIPS, 2 * hours, rows * TILE), F32),
        scratch_shapes=[
            pltpu.VMEM((count + 2 * REACH, 2 * hours, TILE), BF16),
            pltpu.VMEM((hours, sites), F32),
            pltpu.VMEM((count, nb, TILE, TILE), F32),
            pltpu.VMEM((hours, sites), F32),
            pltpu.VMEM((CHIPS, 2 * hours, rows * TILE), F32),
            pltpu.SemaphoreType.DMA((CHIPS + 2,)),
            pltpu.SemaphoreType.DMA((CHIPS,)),
        ],
        compiler_params=params(56),
        cost_estimate=cost(2 * 10**9, 0),
        name="space_wide",
    )(ids, low, high, noise[None, :], x, tiles, right_side)


def space_mixed_kernel(at_ref, ids_ref, left_ref, own_ref, right_ref, weights_ref, out_ref, hi_ref, lo_ref, *refs):
    left_here, own_here, right_here, weights_here, sems = refs
    chips, hours, sites = own_ref.shape
    rows, nb = weights_ref.shape[:2]
    pairs = ((own_ref, own_here), (left_ref, left_here), (right_ref, right_here), (weights_ref, weights_here))
    copies = [pltpu.make_async_copy(source, target, sems.at[k]) for k, (source, target) in enumerate(pairs)]
    for copy in copies:
        copy.start()

    def keep(i, piece):
        high, low = halves(piece.reshape(-1, TILE))
        hi_ref[i] = high
        lo_ref[i] = low

    copies[0].wait()
    for i in range(rows):
        keep(i + REACH, own_here[:, :, i * TILE : (i + 1) * TILE])
    copies[1].wait()
    copies[2].wait()
    for i in range(REACH):
        keep(i, left_here[:, :, i * TILE : (i + 1) * TILE])
        keep(i + rows + REACH, right_here[:, :, i * TILE : (i + 1) * TILE])
    copies[3].wait()
    for row in range(rows):
        places = [ids_ref[n, at_ref[5] * rows + row] - at_ref[2] for n in range(nb)]
        high = jnp.concatenate([hi_ref[i] for i in places], axis=1)
        low = jnp.concatenate([lo_ref[i] for i in places], axis=1)
        weights = jnp.concatenate([weights_here[row, n] for n in range(nb)], axis=1)
        both = dot_nt(high, weights)
        product = both[:, :TILE] + (both[:, TILE:] + dot_nt(low, weights[:TILE]))
        out_ref[:, :, row * TILE : (row + 1) * TILE] = product.reshape(chips, hours, TILE)


def space_mixed(at, ids, left, own, right, weights):
    rows, hours = weights.shape[0], own.shape[0] * own.shape[1]
    return pl.pallas_call(
        space_mixed_kernel,
        in_specs=[SMEM, SMEM, ANY, HBM, ANY, ANY],
        out_specs=VMEM,
        out_shape=jax.ShapeDtypeStruct(own.shape, F32),
        scratch_shapes=[pltpu.VMEM((rows + 2 * REACH, hours, TILE), BF16)] * 2
        + [pltpu.VMEM(a.shape, a.dtype) for a in (left, own, right, weights)]
        + [pltpu.SemaphoreType.DMA((4,))],
        compiler_params=params(24),
        cost_estimate=cost(4000000000, 0),
        name="space_mixed",
    )(at, ids, left, own, right, weights)


def time_rows_kernel(at_ref, *refs):
    strips, (hi_ref, lo_ref) = refs[:SIDE], refs[SIDE:]
    chips, rows, _ = strips[0].shape
    for k in range(SIDE):
        row = pl.multiple_of((at_ref[4] + k) % SIDE * rows, rows)
        for j in range(chips):
            chip = (at_ref[0] + ORIGIN[j]) % chips
            high, low = halves(strips[k][j])
            hi_ref[chip, pl.ds(row, rows), :] = high
            lo_ref[chip, pl.ds(row, rows), :] = low


def time_rows(at, strips):
    chips, rows, depth = strips[0].shape
    shape = jax.ShapeDtypeStruct((chips, rows * SIDE, depth), BF16)
    return pl.pallas_call(
        time_rows_kernel,
        in_specs=[SMEM] + [VMEM] * SIDE,
        out_specs=(VMEM, VMEM),
        out_shape=(shape, shape),
        compiler_params=params(16),
        cost_estimate=cost(0, 0),
        name="time_rows",
    )(at, *strips)


def split_hours(at_ref, own_ref, other_ref, uhi_ref, ulo_ref):
    hours = other_ref.shape[1]
    for chip in range(CHIPS):
        for ref, core in ((own_ref, at_ref[1]), (other_ref, 1 - at_ref[1])):
            row = pl.multiple_of((2 * chip + core) * hours, hours)
            high, low = halves(ref[chip, :hours, :])
            uhi_ref[pl.ds(row, hours), :] = high
            ulo_ref[pl.ds(row, hours), :] = low


def time_product(khi_ref, klo_ref, uhi_ref, ulo_ref, columns):
    chips, hours, depth = khi_ref.shape
    khi = khi_ref[...].reshape(chips * hours, depth)
    klo = klo_ref[...].reshape(chips * hours, depth)
    uhi, ulo = uhi_ref[:, columns], ulo_ref[:, columns]
    mixed = dot_nn(khi, uhi) + (dot_nn(khi, ulo) + dot_nn(klo, uhi))
    return mixed.reshape(chips, hours, -1)


def residual_kernel(at_ref, khi_ref, klo_ref, got_ref, other_ref, out_ref, uhi_ref, ulo_ref):
    chips, hours, sites = out_ref.shape
    split_hours(at_ref, got_ref, other_ref, uhi_ref, ulo_ref)
    width = sites // 2
    for part in range(2):
        columns = slice(part * width, (part + 1) * width)
        mixed = time_product(khi_ref, klo_ref, uhi_ref, ulo_ref, columns)
        out_ref[:, :, columns] = got_ref[:, hours:, columns] - mixed


def residual_of(at, khi, klo, got, other):
    chips, hours, sites = other.shape
    return pl.pallas_call(
        residual_kernel,
        in_specs=[SMEM] + [VMEM] * 4,
        out_specs=VMEM,
        out_shape=jax.ShapeDtypeStruct(other.shape, F32),
        scratch_shapes=[pltpu.VMEM((2 * chips * hours, sites), BF16)] * 2,
        compiler_params=params(24),
        cost_estimate=cost(0, 0),
        name="residual_of",
    )(at, khi, klo, got, other)


def image_kernel(at_ref, khi_ref, klo_ref, own_ref, other_ref, r_ref, noise_ref, out_ref, sums_ref, uhi_ref, ulo_ref):
    chips, hours, sites = own_ref.shape
    split_hours(at_ref, own_ref, other_ref, uhi_ref, ulo_ref)
    width = sites // 2
    squares = jnp.zeros((8, TILE), F32)
    curves = jnp.zeros((8, TILE), F32)
    for part in range(2):
        columns = slice(part * width, (part + 1) * width)
        mixed = time_product(khi_ref, klo_ref, uhi_ref, ulo_ref, columns)
        r = r_ref[:, :, columns]
        image = mixed + noise_ref[:, columns][None] * r
        out_ref[:, :, columns] = image
        for t in range(width // TILE):
            piece = slice(t * TILE, (t + 1) * TILE)
            a, b = r[:, :, piece].reshape(-1, 8, TILE), image[:, :, piece].reshape(-1, 8, TILE)
            squares += jnp.sum(a * a, axis=0)
            curves += jnp.sum(a * b, axis=0)
    sums_ref[:8, :] = squares
    sums_ref[8:, :] = curves


def image_of(at, khi, klo, own, other, residual, noise):
    chips, hours, sites = own.shape
    return pl.pallas_call(
        image_kernel,
        in_specs=[SMEM] + [VMEM] * 6,
        out_specs=[VMEM] * 2,
        out_shape=[jax.ShapeDtypeStruct(own.shape, F32), jax.ShapeDtypeStruct((16, TILE), F32)],
        scratch_shapes=[pltpu.VMEM((2 * chips * hours, sites), BF16)] * 2,
        compiler_params=params(24),
        cost_estimate=cost(0, 0),
        name="image_of",
    )(at, khi, klo, own, other, residual, noise)


def update_kernel(at_ref, start_ref, residual_ref, image_ref, *refs):
    sums, (iterate_ref, next_ref) = refs[:-2], refs[-2:]
    chips, _, width = residual_ref.shape
    total = sums[0][...]
    for part in sums[1:]:
        total += part[...]
    alpha = jnp.sum(total[:8, :]) / jnp.sum(total[8:, :])
    for g in range(chips):
        columns = slice(g * width, (g + 1) * width)
        chip = turned(at_ref[6], g)
        r = residual_ref[chip]
        iterate_ref[:, columns] = start_ref[:, columns] + alpha * r
        next_ref[:, columns] = r - alpha * image_ref[chip]


def update(at, start, residual, image, sums):
    shape = jax.ShapeDtypeStruct(start.shape, F32)
    return pl.pallas_call(
        update_kernel,
        in_specs=[SMEM] + [VMEM] * (3 + len(sums)),
        out_specs=(VMEM, VMEM),
        out_shape=(shape, shape),
        compiler_params=params(24),
        cost_estimate=cost(0, 0),
        name="update",
    )(at, start, residual, image, *sums)


def first_rows_kernel(value_ref, *refs):
    refs[-1][...] = value_ref[:, : refs[-1].shape[1], :]


def first_rows(value, rows, after):
    return pl.pallas_call(
        first_rows_kernel,
        in_specs=[VMEM] + [ANY] * len(after),
        out_specs=VMEM,
        out_shape=jax.ShapeDtypeStruct((value.shape[0], rows, value.shape[2]), F32),
        compiler_params=params(16),
        cost_estimate=cost(0, 0),
        name="first_rows",
    )(value, *after)


def ordered(value, *after):
    return pl.pallas_call(
        lambda *refs: None,
        in_specs=[ANY] + [VMEM] * len(after),
        out_specs=ANY,
        out_shape=jax.ShapeDtypeStruct(value.shape, value.dtype),
        input_output_aliases={0: 0},
        cost_estimate=cost(0, 0),
        name="ordered",
    )(value, *after)


def joined(arrays, after):
    def kernel(*refs):
        first = 0
        for ref in refs[: len(arrays)]:
            refs[-1][first : first + ref.shape[0]] = ref[...]
            first += ref.shape[0]

    return pl.pallas_call(
        kernel,
        in_specs=[VMEM] * (len(arrays) + len(after)),
        out_specs=VMEM,
        out_shape=jax.ShapeDtypeStruct((sum(a.shape[0] for a in arrays),) + arrays[0].shape[1:], F32),
        compiler_params=params(8),
        cost_estimate=cost(0, 0),
        name="joined",
    )(*arrays, *after)


def copied_kernel(value_ref, out_ref, sem):
    copy = pltpu.make_async_copy(value_ref, out_ref, sem)
    copy.start()
    copy.wait()


def copied(value):
    return pl.pallas_call(
        copied_kernel,
        in_specs=[VMEM],
        out_specs=ANY,
        out_shape=jax.ShapeDtypeStruct(value.shape, value.dtype),
        scratch_shapes=[pltpu.SemaphoreType.DMA],
        compiler_params=params(16),
        cost_estimate=cost(0, 0),
        name="copied",
    )(value)


def token(value):
    return value.reshape((-1,) + value.shape[-2:])[0, :16, :TILE]


def exchange(blocks):
    return lax.all_to_all(blocks, "tm", 0, 0, axis_index_groups=SAME_CORE, tiled=True)


def along_side(shift, axis):
    place = lambda a, b: a * SIDE + b
    if axis == "y":
        return [(place(a, b), place(a, (b + shift) % SIDE)) for a in range(SIDE) for b in range(SIDE)]
    return [(place(a, b), place((a + shift) % SIDE, b)) for a in range(SIDE) for b in range(SIDE)]


def local(start, right_side, noise, tile_ids, space_tiles, time_kernel):
    hours_dev, sites_dev = start.shape
    count = tile_ids.shape[0]
    width = sites_dev // CHIPS
    edge = REACH * TILE
    spaces = lax.axis_size("space")
    space, tm = lax.axis_index("space"), lax.axis_index("tm")
    chip, core = tm // 2, tm % 2
    base = space * count - REACH
    group = turned(space, chip)
    at = jnp.stack([chip, core, base + group * (count // CHIPS), base, space % SIDE, group, space]).astype(jnp.int32)

    forward = [(i, i + 1) for i in range(spaces - 1)]
    backward = [(target, source) for source, target in forward]
    low = lax.ppermute(start[:, sites_dev - edge :], "space", forward)
    high = lax.ppermute(start[:, :edge], "space", backward)
    rows = time_kernel.shape[0] // SIDE
    ids = tile_ids.T
    strip = lax.dynamic_slice(time_kernel, (space % SIDE * rows, 0), (rows, time_kernel.shape[1]))[None]
    strip = joined([strip, lax.ppermute(strip, "tm", along_z(CHIPS // 2))], [])
    beside = [lax.ppermute(strip, "tm", along_z(shift)) for shift in (-1, 1, 2)]
    sent = space_wide(ids, low, high, start, space_tiles, right_side, noise)
    strip = joined([strip] + beside, [])
    strips = [strip] + [lax.ppermute(strip, "space", along_side(-k, "y")) for k in range(1, SIDE)]
    khi, klo = time_rows(at, strips)
    weights = weights_of(at, space_tiles)

    got = exchange(ordered(sent, sum(token(b) for b in beside)))
    other = lax.ppermute(first_rows(got, hours_dev, [token(khi), token(weights)]), "tm", SWAP)
    residual = residual_of(at, khi, klo, got, other)

    up, down = [], []
    line = [s * CHIPS + (CHIPS - 1 - g if s % 2 else g) for s in range(spaces) for g in range(CHIPS)]
    for source, target in zip(line, line[1:]):
        for c in range(2):
            up.append((source * 2 + c, target * 2 + c))
            down.append((target * 2 + c, source * 2 + c))
    left = lax.ppermute(residual[:, :, width - edge :], ("space", "tm"), up)
    right = lax.ppermute(residual[:, :, :edge], ("space", "tm"), down)
    kept = copied(residual)
    back_r = exchange(kept)
    mixed = space_mixed(at, ids, left, kept, right, weights)
    other = lax.ppermute(mixed, "tm", SWAP)
    noise_here = lax.dynamic_slice(noise, (group * width,), (width,))[None, :]
    image, sums = image_of(at, khi, klo, mixed, other, residual, noise_here)
    sums = sums + lax.ppermute(sums, "tm", SWAP)
    far = lax.ppermute(sums, "tm", along_z(CHIPS // 2))
    back_p = exchange(ordered(image, far))
    sums = sums + far
    for axis in ("y", "x"):
        sums = sum([lax.ppermute(sums, "space", along_side(shift, axis)) for shift in range(1, SIDE)], sums)
    sums = [sums] + [lax.ppermute(sums, "tm", along_z(shift)) for shift in range(1, CHIPS // 2)]
    return update(at, start, back_r, back_p, sums)


def solution(mesh):
    placed = (
        P("tm", "space"),
        P("tm", "space"),
        P("space"),
        P("space", None),
        P("space", None, None, None),
        P("tm", None),
    )
    return jax.shard_map(
        local,
        mesh=mesh,
        in_specs=placed,
        out_specs=(P("tm", "space"), P("tm", "space")),
        check_vma=False,
    )
```

```python
import jax
import jax.numpy as jnp
from jax import lax
from jax.experimental import pallas as pl
from jax.experimental.pallas import tpu as pltpu
from jax.sharding import PartitionSpec as P

REACH = 2
TILE = 128
CHIPS = 8
SAME_CORE = [[chip * 2 + core for chip in range(CHIPS)] for core in range(2)]
SIDE = 4
ORIGIN = (0, 4, 1, 5, 7, 3, 6, 2)
SWAP = [(i, i ^ 1) for i in range(2 * CHIPS)]
F32 = jnp.float32
BF16 = jnp.bfloat16
VMEM = pl.BlockSpec(memory_space=pltpu.VMEM)
SMEM = pl.BlockSpec(memory_space=pltpu.SMEM)
ANY = pl.BlockSpec(memory_space=pl.ANY)
HBM = pl.BlockSpec(memory_space=pltpu.HBM)


def along_z(shift):
    return [(z * 2 + c, (z + shift) % CHIPS * 2 + c) for z in range(CHIPS) for c in range(2)]


def halves(value):
    high = value.astype(BF16)
    return high, (value - high.astype(F32)).astype(BF16)


def turned(space, index):
    return jnp.where(space % 2 == 1, CHIPS - 1 - index, index)


def params(megabytes):
    return pltpu.CompilerParams(vmem_limit_bytes=megabytes * 1024 * 1024)


def cost(flops, moved):
    return pl.CostEstimate(flops=flops, bytes_accessed=moved, transcendentals=0)


def dot_nt(a, b):
    return lax.dot_general(a, b, (((1,), (1,)), ((), ())), preferred_element_type=F32)


def dot_nn(a, b):
    return lax.dot_general(a, b, (((1,), (0,)), ((), ())), preferred_element_type=F32)


def stacked_halves(tiles):
    high, low = halves(tiles)
    return jnp.concatenate([high, low], axis=-2)


def weights_kernel(at_ref, tiles_ref, out_ref):
    out_ref[...] = stacked_halves(tiles_ref[...])


def weights_of(at, tiles):
    count, nb = tiles.shape[:2]
    rows = count // CHIPS
    return pl.pallas_call(
        weights_kernel,
        grid_spec=pltpu.PrefetchScalarGridSpec(
            num_scalar_prefetch=1,
            grid=(rows,),
            in_specs=[pl.BlockSpec((1, nb, TILE, TILE), lambda i, at: (at[5] * rows + i, 0, 0, 0))],
            out_specs=pl.BlockSpec((1, nb, 2 * TILE, TILE), lambda i, at: (i, 0, 0, 0)),
        ),
        out_shape=jax.ShapeDtypeStruct((rows, nb, 2 * TILE, TILE), BF16),
        compiler_params=params(56),
        cost_estimate=cost(0, 0),
        name="weights_of",
    )(at, tiles)


def space_wide_kernel(ids_ref, low_ref, high_ref, noise_ref, x_ref, tiles_ref, right_ref, *refs):
    out_ref, win_ref, x_here, tile_ref, right_here, stage_ref, sems, out_sems = refs
    hours, sites = x_ref.shape
    space = lax.axis_index("space")
    groups = stage_ref.shape[0]
    rows, nb = tile_ref.shape[0] // groups, tile_ref.shape[1]
    width = rows * TILE
    count = sites // TILE
    base = space * count - REACH
    place = lambda g: slice(g * width, (g + 1) * width)
    x_copy = pltpu.make_async_copy(x_ref, x_here, sems.at[groups])
    right_copy = pltpu.make_async_copy(right_ref, right_here, sems.at[groups + 1])
    tiles = [
        pltpu.make_async_copy(tiles_ref.at[pl.ds(g * rows, rows)], tile_ref.at[pl.ds(g * rows, rows)], sems.at[g])
        for g in range(groups)
    ]
    x_copy.start()
    tiles[0].start()
    right_copy.start()
    for copy in tiles[1:]:
        copy.start()

    def keep(i, piece):
        high, low = halves(piece)
        win_ref[i, :hours, :] = high
        win_ref[i, hours:, :] = low

    for i in range(REACH):
        keep(i, low_ref[:, i * TILE : (i + 1) * TILE])
        keep(i + count + REACH, high_ref[:, i * TILE : (i + 1) * TILE])
    x_copy.wait()
    for i in range(count):
        keep(i + REACH, x_here[:, i * TILE : (i + 1) * TILE])
    sent = []
    for g in range(groups):
        tiles[g].wait()
        for i in range(rows):
            row = g * rows + i
            field = [win_ref[ids_ref[n, row] - base] for n in range(nb)]
            mine = jnp.concatenate([tile_ref[row, n] for n in range(nb)], axis=1)
            product = dot_nt(jnp.concatenate(field, axis=1), stacked_halves(mine))
            columns = slice(i * TILE, (i + 1) * TILE)
            stage_ref[g, :hours, columns] = product[:hours, :TILE] + (product[:hours, TILE:] + product[hours:, :TILE])
        if g == 0:
            right_copy.wait()
        stage_ref[g, hours:, :] = right_here[:, place(g)] - noise_ref[:, place(g)] * x_here[:, place(g)]
        sent.append(pltpu.make_async_copy(stage_ref.at[g], out_ref.at[turned(space, g)], out_sems.at[g]))
        sent[-1].start()
    for copy in sent:
        copy.wait()


def space_wide(ids, low, high, x, tiles, right_side, noise):
    hours, sites = x.shape
    nb, count = ids.shape
    rows = count // CHIPS
    return pl.pallas_call(
        space_wide_kernel,
        in_specs=[SMEM] + [VMEM] * 3 + [HBM] * 3,
        out_specs=ANY,
        out_shape=jax.ShapeDtypeStruct((CHIPS, 2 * hours, rows * TILE), F32),
        scratch_shapes=[
            pltpu.VMEM((count + 2 * REACH, 2 * hours, TILE), BF16),
            pltpu.VMEM((hours, sites), F32),
            pltpu.VMEM((count, nb, TILE, TILE), F32),
            pltpu.VMEM((hours, sites), F32),
            pltpu.VMEM((CHIPS, 2 * hours, rows * TILE), F32),
            pltpu.SemaphoreType.DMA((CHIPS + 2,)),
            pltpu.SemaphoreType.DMA((CHIPS,)),
        ],
        compiler_params=params(56),
        cost_estimate=cost(2 * 10**9, 0),
        name="space_wide",
    )(ids, low, high, noise[None, :], x, tiles, right_side)


def space_mixed_kernel(at_ref, ids_ref, left_ref, own_ref, right_ref, weights_ref, out_ref, hi_ref, lo_ref, *refs):
    left_here, own_here, right_here, weights_here, sems = refs
    chips, hours, sites = own_ref.shape
    rows, nb = weights_ref.shape[:2]
    pairs = ((own_ref, own_here), (left_ref, left_here), (right_ref, right_here), (weights_ref, weights_here))
    copies = [pltpu.make_async_copy(source, target, sems.at[k]) for k, (source, target) in enumerate(pairs)]
    for copy in copies:
        copy.start()

    def keep(i, piece):
        high, low = halves(piece.reshape(-1, TILE))
        hi_ref[i] = high
        lo_ref[i] = low

    copies[0].wait()
    for i in range(rows):
        keep(i + REACH, own_here[:, :, i * TILE : (i + 1) * TILE])
    copies[1].wait()
    copies[2].wait()
    for i in range(REACH):
        keep(i, left_here[:, :, i * TILE : (i + 1) * TILE])
        keep(i + rows + REACH, right_here[:, :, i * TILE : (i + 1) * TILE])
    copies[3].wait()
    for row in range(rows):
        places = [ids_ref[n, at_ref[5] * rows + row] - at_ref[2] for n in range(nb)]
        high = jnp.concatenate([hi_ref[i] for i in places], axis=1)
        low = jnp.concatenate([lo_ref[i] for i in places], axis=1)
        weights = jnp.concatenate([weights_here[row, n] for n in range(nb)], axis=1)
        both = dot_nt(high, weights)
        product = both[:, :TILE] + (both[:, TILE:] + dot_nt(low, weights[:TILE]))
        out_ref[:, :, row * TILE : (row + 1) * TILE] = product.reshape(chips, hours, TILE)


def space_mixed(at, ids, left, own, right, weights):
    rows, hours = weights.shape[0], own.shape[0] * own.shape[1]
    return pl.pallas_call(
        space_mixed_kernel,
        in_specs=[SMEM, SMEM, ANY, HBM, ANY, ANY],
        out_specs=VMEM,
        out_shape=jax.ShapeDtypeStruct(own.shape, F32),
        scratch_shapes=[pltpu.VMEM((rows + 2 * REACH, hours, TILE), BF16)] * 2
        + [pltpu.VMEM(a.shape, a.dtype) for a in (left, own, right, weights)]
        + [pltpu.SemaphoreType.DMA((4,))],
        compiler_params=params(24),
        cost_estimate=cost(4000000000, 0),
        name="space_mixed",
    )(at, ids, left, own, right, weights)


def time_rows_kernel(at_ref, *refs):
    strips, (hi_ref, lo_ref) = refs[:SIDE], refs[SIDE:]
    chips, rows, _ = strips[0].shape
    for k in range(SIDE):
        row = pl.multiple_of((at_ref[4] + k) % SIDE * rows, rows)
        for j in range(chips):
            chip = (at_ref[0] + ORIGIN[j]) % chips
            high, low = halves(strips[k][j])
            hi_ref[chip, pl.ds(row, rows), :] = high
            lo_ref[chip, pl.ds(row, rows), :] = low


def time_rows(at, strips):
    chips, rows, depth = strips[0].shape
    shape = jax.ShapeDtypeStruct((chips, rows * SIDE, depth), BF16)
    return pl.pallas_call(
        time_rows_kernel,
        in_specs=[SMEM] + [VMEM] * SIDE,
        out_specs=(VMEM, VMEM),
        out_shape=(shape, shape),
        compiler_params=params(16),
        cost_estimate=cost(0, 0),
        name="time_rows",
    )(at, *strips)


def split_hours(at_ref, own_ref, other_ref, uhi_ref, ulo_ref):
    hours = other_ref.shape[1]
    for chip in range(CHIPS):
        for ref, core in ((own_ref, at_ref[1]), (other_ref, 1 - at_ref[1])):
            row = pl.multiple_of((2 * chip + core) * hours, hours)
            high, low = halves(ref[chip, :hours, :])
            uhi_ref[pl.ds(row, hours), :] = high
            ulo_ref[pl.ds(row, hours), :] = low


def time_product(khi_ref, klo_ref, uhi_ref, ulo_ref, columns):
    chips, hours, depth = khi_ref.shape
    khi = khi_ref[...].reshape(chips * hours, depth)
    klo = klo_ref[...].reshape(chips * hours, depth)
    uhi, ulo = uhi_ref[:, columns], ulo_ref[:, columns]
    mixed = dot_nn(khi, uhi) + (dot_nn(khi, ulo) + dot_nn(klo, uhi))
    return mixed.reshape(chips, hours, -1)


def residual_kernel(at_ref, khi_ref, klo_ref, got_ref, other_ref, out_ref, uhi_ref, ulo_ref):
    chips, hours, sites = out_ref.shape
    split_hours(at_ref, got_ref, other_ref, uhi_ref, ulo_ref)
    width = sites // 2
    for part in range(2):
        columns = slice(part * width, (part + 1) * width)
        mixed = time_product(khi_ref, klo_ref, uhi_ref, ulo_ref, columns)
        out_ref[:, :, columns] = got_ref[:, hours:, columns] - mixed


def residual_of(at, khi, klo, got, other):
    chips, hours, sites = other.shape
    return pl.pallas_call(
        residual_kernel,
        in_specs=[SMEM] + [VMEM] * 4,
        out_specs=VMEM,
        out_shape=jax.ShapeDtypeStruct(other.shape, F32),
        scratch_shapes=[pltpu.VMEM((2 * chips * hours, sites), BF16)] * 2,
        compiler_params=params(24),
        cost_estimate=cost(0, 0),
        name="residual_of",
    )(at, khi, klo, got, other)


def image_kernel(at_ref, khi_ref, klo_ref, own_ref, other_ref, r_ref, noise_ref, out_ref, sums_ref, uhi_ref, ulo_ref):
    chips, hours, sites = own_ref.shape
    split_hours(at_ref, own_ref, other_ref, uhi_ref, ulo_ref)
    width = sites // 2
    squares = jnp.zeros((8, TILE), F32)
    curves = jnp.zeros((8, TILE), F32)
    for part in range(2):
        columns = slice(part * width, (part + 1) * width)
        mixed = time_product(khi_ref, klo_ref, uhi_ref, ulo_ref, columns)
        r = r_ref[:, :, columns]
        image = mixed + noise_ref[:, columns][None] * r
        out_ref[:, :, columns] = image
        for t in range(width // TILE):
            piece = slice(t * TILE, (t + 1) * TILE)
            a, b = r[:, :, piece].reshape(-1, 8, TILE), image[:, :, piece].reshape(-1, 8, TILE)
            squares += jnp.sum(a * a, axis=0)
            curves += jnp.sum(a * b, axis=0)
    sums_ref[:8, :] = squares
    sums_ref[8:, :] = curves


def image_of(at, khi, klo, own, other, residual, noise):
    chips, hours, sites = own.shape
    return pl.pallas_call(
        image_kernel,
        in_specs=[SMEM] + [VMEM] * 6,
        out_specs=[VMEM] * 2,
        out_shape=[jax.ShapeDtypeStruct(own.shape, F32), jax.ShapeDtypeStruct((16, TILE), F32)],
        scratch_shapes=[pltpu.VMEM((2 * chips * hours, sites), BF16)] * 2,
        compiler_params=params(24),
        cost_estimate=cost(0, 0),
        name="image_of",
    )(at, khi, klo, own, other, residual, noise)


def update_kernel(at_ref, start_ref, residual_ref, image_ref, *refs):
    sums, (iterate_ref, next_ref) = refs[:-2], refs[-2:]
    chips, _, width = residual_ref.shape
    total = sums[0][...]
    for part in sums[1:]:
        total += part[...]
    alpha = jnp.sum(total[:8, :]) / jnp.sum(total[8:, :])
    for g in range(chips):
        columns = slice(g * width, (g + 1) * width)
        chip = turned(at_ref[6], g)
        r = residual_ref[chip]
        iterate_ref[:, columns] = start_ref[:, columns] + alpha * r
        next_ref[:, columns] = r - alpha * image_ref[chip]


def update(at, start, residual, image, sums):
    shape = jax.ShapeDtypeStruct(start.shape, F32)
    return pl.pallas_call(
        update_kernel,
        in_specs=[SMEM] + [VMEM] * (3 + len(sums)),
        out_specs=(VMEM, VMEM),
        out_shape=(shape, shape),
        compiler_params=params(24),
        cost_estimate=cost(0, 0),
        name="update",
    )(at, start, residual, image, *sums)


def first_rows_kernel(value_ref, *refs):
    refs[-1][...] = value_ref[:, : refs[-1].shape[1], :]


def first_rows(value, rows, after):
    return pl.pallas_call(
        first_rows_kernel,
        in_specs=[VMEM] + [ANY] * len(after),
        out_specs=VMEM,
        out_shape=jax.ShapeDtypeStruct((value.shape[0], rows, value.shape[2]), F32),
        compiler_params=params(16),
        cost_estimate=cost(0, 0),
        name="first_rows",
    )(value, *after)


def ordered(value, *after):
    return pl.pallas_call(
        lambda *refs: None,
        in_specs=[ANY] + [VMEM] * len(after),
        out_specs=ANY,
        out_shape=jax.ShapeDtypeStruct(value.shape, value.dtype),
        input_output_aliases={0: 0},
        cost_estimate=cost(0, 0),
        name="ordered",
    )(value, *after)


def joined(arrays, after):
    def kernel(*refs):
        first = 0
        for ref in refs[: len(arrays)]:
            refs[-1][first : first + ref.shape[0]] = ref[...]
            first += ref.shape[0]

    return pl.pallas_call(
        kernel,
        in_specs=[VMEM] * (len(arrays) + len(after)),
        out_specs=VMEM,
        out_shape=jax.ShapeDtypeStruct((sum(a.shape[0] for a in arrays),) + arrays[0].shape[1:], F32),
        compiler_params=params(8),
        cost_estimate=cost(0, 0),
        name="joined",
    )(*arrays, *after)


def copied_kernel(value_ref, out_ref, sem):
    copy = pltpu.make_async_copy(value_ref, out_ref, sem)
    copy.start()
    copy.wait()


def copied(value):
    return pl.pallas_call(
        copied_kernel,
        in_specs=[VMEM],
        out_specs=ANY,
        out_shape=jax.ShapeDtypeStruct(value.shape, value.dtype),
        scratch_shapes=[pltpu.SemaphoreType.DMA],
        compiler_params=params(16),
        cost_estimate=cost(0, 0),
        name="copied",
    )(value)


def token(value):
    return value.reshape((-1,) + value.shape[-2:])[0, :16, :TILE]


def exchange(blocks):
    return lax.all_to_all(blocks, "tm", 0, 0, axis_index_groups=SAME_CORE, tiled=True)


def along_side(shift, axis):
    place = lambda a, b: a * SIDE + b
    if axis == "y":
        return [(place(a, b), place(a, (b + shift) % SIDE)) for a in range(SIDE) for b in range(SIDE)]
    return [(place(a, b), place((a + shift) % SIDE, b)) for a in range(SIDE) for b in range(SIDE)]


def local(start, right_side, noise, tile_ids, space_tiles, time_kernel):
    hours_dev, sites_dev = start.shape
    count = tile_ids.shape[0]
    width = sites_dev // CHIPS
    edge = REACH * TILE
    spaces = lax.axis_size("space")
    space, tm = lax.axis_index("space"), lax.axis_index("tm")
    chip, core = tm // 2, tm % 2
    base = space * count - REACH
    group = turned(space, chip)
    at = jnp.stack([chip, core, base + group * (count // CHIPS), base, space % SIDE, group, space]).astype(jnp.int32)

    forward = [(i, i + 1) for i in range(spaces - 1)]
    backward = [(target, source) for source, target in forward]
    low = lax.ppermute(start[:, sites_dev - edge :], "space", forward)
    high = lax.ppermute(start[:, :edge], "space", backward)
    rows = time_kernel.shape[0] // SIDE
    ids = tile_ids.T
    strip = lax.dynamic_slice(time_kernel, (space % SIDE * rows, 0), (rows, time_kernel.shape[1]))[None]
    strip = joined([strip, lax.ppermute(strip, "tm", along_z(CHIPS // 2))], [])
    beside = [lax.ppermute(strip, "tm", along_z(shift)) for shift in (-1, 1, 2)]
    sent = space_wide(ids, low, high, start, space_tiles, right_side, noise)
    strip = joined([strip] + beside, [])
    strips = [strip] + [lax.ppermute(strip, "space", along_side(-k, "y")) for k in range(1, SIDE)]
    khi, klo = time_rows(at, strips)
    weights = weights_of(at, space_tiles)

    got = exchange(ordered(sent, sum(token(b) for b in beside)))
    other = lax.ppermute(first_rows(got, hours_dev, [token(khi), token(weights)]), "tm", SWAP)
    residual = residual_of(at, khi, klo, got, other)

    up, down = [], []
    line = [s * CHIPS + (CHIPS - 1 - g if s % 2 else g) for s in range(spaces) for g in range(CHIPS)]
    for source, target in zip(line, line[1:]):
        for c in range(2):
            up.append((source * 2 + c, target * 2 + c))
            down.append((target * 2 + c, source * 2 + c))
    left = lax.ppermute(residual[:, :, width - edge :], ("space", "tm"), up)
    right = lax.ppermute(residual[:, :, :edge], ("space", "tm"), down)
    kept = copied(residual)
    back_r = exchange(kept)
    mixed = space_mixed(at, ids, left, kept, right, weights)
    other = lax.ppermute(mixed, "tm", SWAP)
    noise_here = lax.dynamic_slice(noise, (group * width,), (width,))[None, :]
    image, sums = image_of(at, khi, klo, mixed, other, residual, noise_here)
    far = lax.ppermute(sums, "tm", along_z(CHIPS // 2))
    back_p = exchange(ordered(image, far))
    sums = sums + far
    sums = sums + lax.ppermute(sums, "tm", SWAP)
    for axis in ("y", "x"):
        sums = sum([lax.ppermute(sums, "space", along_side(shift, axis)) for shift in range(1, SIDE)], sums)
    sums = [sums] + [lax.ppermute(sums, "tm", along_z(shift)) for shift in range(1, CHIPS // 2)]
    return update(at, start, back_r, back_p, sums)


def solution(mesh):
    placed = (
        P("tm", "space"),
        P("tm", "space"),
        P("space"),
        P("space", None),
        P("space", None, None, None),
        P("tm", None),
    )
    return jax.shard_map(
        local,
        mesh=mesh,
        in_specs=placed,
        out_specs=(P("tm", "space"), P("tm", "space")),
        check_vma=False,
    )
```
